32 devices in a mesh: dp: 8 (over z, x), expert: 4 (over y, core).
Axes of the slice: x: 2, y: 2, z: 4, core: 2. Of those that a mesh axis runs over, the one named last changes fastest.
Arguments:
- text_embed: bfloat16 [2048, 2048], P(('dp', 'expert')), may hold values from -6 to 6
- image_feats: bfloat16 [1024, 4608], P(('dp', 'expert')), may hold values from -6 to 6
- tile_pos: int32 [1024], P(('dp', 'expert')), may hold values from 0 to 2047, as said below
- proj_in: bfloat16 [4608, 2048], P(None, 'expert'), may hold values from -0.09375 to 0.09375
- proj_out: bfloat16 [2048, 2048], P('expert'), may hold values from -0.125 to 0.125
- norm_gain: float32 [2048], replicated, may hold values from 0.1 to 1.9
- shared_gate: bfloat16 [2048, 2816], P(None, 'expert'), may hold values from -0.125 to 0.125
- shared_up: bfloat16 [2048, 2816], P(None, 'expert'), may hold values from -0.125 to 0.125
- shared_down: bfloat16 [2816, 2048], P('expert'), may hold values from -0.109375 to 0.109375
- expert_gate: bfloat16 [8, 2048, 1408], P('dp', None, 'expert'), may hold values from -0.125 to 0.125
- expert_up: bfloat16 [8, 2048, 1408], P('dp', None, 'expert'), may hold values from -0.125 to 0.125
- expert_down: bfloat16 [8, 1408, 2048], P('dp', 'expert'), may hold values from -0.15625 to 0.15625
- route_ids: int32 [2048, 2], P(('dp', 'expert')), may hold values from 0 to 7, all different within a row; in each aligned block of 256 rows (0 to 255, 256 to 511, ...) at most 96 rows name the same one
- route_wts: int32 [2048, 2], P(('dp', 'expert')), may hold values from 1 to 65535
Outputs:
- block_out: bfloat16 [2048, 2048], P(('dp', 'expert'))
The draws below stay inside these ranges and needn't reach their ends.
Inputs may be any that keep to these rules, and one draw needn't show every extreme that they name: `tile_pos`: positions are distinct. The 32 image tokens of one device go 4 to each index of dp, always to rows held by the devices with the sender's own index of expert. `route_ids`: in each aligned block of 256 rows no expert is named by more than 96 rows, a bound that some block reaches.
All inputs are finite; a program needn't handle non-finite values.
Results may differ from the reference program's by a relative error of at most 0.018.
Values may be sent and summed in bfloat16 or wider, within the bound.
No kernel may reach another device: no remote copies, remote signals or barrier semaphores. Data moves between devices by JAX's collectives and lax.ppermute only.
A program may use at most 128 MiB of HBM per device.

```python
import math
import jax
import jax.numpy as jnp
import numpy as np
from jax import lax

D = 2048
VIS = 4608
FF = 1408
FFS = 2816
TOP = 2
TOK_DEV = 64
IMG_DEV = 32
EXPERTS = 8
GROUP_TOK = 256
CAP = 96
TOKENS = 2048
IMG_TOKENS = 1024
N_DP = 8
N_EXPERT = 4


def draw_tile_pos(key, part):
    peer = IMG_DEV // N_DP
    ndev = N_DP * N_EXPERT
    key_a = jax.random.fold_in(key, 11)
    key_b = jax.random.fold_in(key, 12)
    chosen = jax.vmap(lambda k: jax.random.permutation(k, TOK_DEV))(jax.random.split(key_a, ndev))[:, :IMG_DEV]
    chosen = chosen.astype(jnp.int32).reshape(N_DP, N_EXPERT, N_DP, peer)
    base = (jnp.arange(N_DP, dtype=jnp.int32)[:, None] * N_EXPERT + jnp.arange(N_EXPERT, dtype=jnp.int32)[None, :]) * TOK_DEV
    position = chosen + base[:, :, None, None]
    position = jnp.transpose(position, (2, 1, 0, 3)).reshape(ndev, IMG_DEV)
    shuffle = jax.vmap(lambda k: jax.random.permutation(k, IMG_DEV))(jax.random.split(key_b, ndev))
    position = jnp.take_along_axis(position, shuffle.astype(jnp.int32), axis=1)
    return position.reshape(-1).astype(jnp.int32)


def plant(values, stream_key, low, top_value):
    extent = values.shape
    index_at = [jax.random.randint(jax.random.fold_in(stream_key, axis), (), 0, extent[axis]) for axis in range(len(extent))]
    values = values.at[tuple(index_at)].set(low)
    longest = extent.index(max(extent))
    index_at[longest] = (index_at[longest] + 1) % extent[longest]
    return values.at[tuple(index_at)].set(top_value)


def shard_levels(key, shape, cuts, smallest, high):
    factor_of, own = 1.0, jax.random.fold_in(key, 6)
    for dim, shards_of in cuts:
        heights = jnp.exp(jax.random.uniform(jax.random.fold_in(own, dim), (shards_of,), jnp.float32, smallest / len(cuts), high / len(cuts)))
        factor_of = factor_of * jnp.repeat(heights, shape[dim] // shards_of).reshape([-1 if axis == dim else 1 for axis in range(len(shape))])
    return factor_of


def routed_block(key, own, number, rows, number_of, top, reach, slope):
    sequence = jax.random.permutation(key, number_of)
    crowded, common = load_shares(number_of, rows * top, reach, slope, True), load_shares(number_of, rows * top, reach, slope, False)
    places = jnp.arange(number_of)

    def named(sizes, rotation):
        used = int((sizes > 0).sum())
        fixed = max(1, used // 4)
        passed = fixed + (places - fixed + rotation * (used - fixed)) % max(1, number_of - fixed)
        return jnp.zeros((number_of,), jnp.int32).at[sequence[jnp.where(places < fixed, places, passed)]].set(jnp.asarray(sizes, jnp.int32))

    sizes = jnp.where(number % 4 == 0, named(crowded, number // 4), named(common, number - number // 4 - 1))
    mixed = jax.random.permutation(jax.random.fold_in(own, 3), number_of)
    giver, receiver = mixed[0:number_of // 2 * 2:2], mixed[1:number_of // 2 * 2:2]
    margin = jnp.minimum(sizes[giver] - 1, reach - sizes[receiver]) // 2
    margin = jnp.where((giver == sequence[0]) | (receiver == sequence[0]) | (sizes[receiver] == 0), 0, jnp.maximum(margin, 0))
    passed = jax.random.randint(jax.random.fold_in(own, 4), (number_of // 2,), 0, 1 << 20) % (margin + 1)
    sizes = sizes.at[giver].add(-passed).at[receiver].add(passed)
    members = jnp.searchsorted(jnp.cumsum(sizes), jnp.arange(rows * top), side="right").astype(jnp.int32)
    listing = members.reshape(top, rows).T
    listing = listing[jax.random.permutation(jax.random.fold_in(own, 1), rows)]
    rotation = jax.random.randint(jax.random.fold_in(own, 2), (rows, 1), 0, top)
    return jnp.take_along_axis(listing, (jnp.arange(top)[None, :] + rotation) % top, axis=1)


def load_shares(count, total, limit, lean, full):
    loads = [(1 << 20) // math.isqrt(rank ** lean) + 1 for rank in range(1, count + 1)]
    largest = limit if full else min(limit, max(-(-total // count), total * loads[0] // sum(loads)))
    least = 1 if total - largest >= count - 1 else 0
    counts, rest = [largest] + [least] * (count - 1), total - largest - least * (count - 1)
    while rest > 0:
        free = [i for i in range(1, count) if counts[i] < largest] or [i for i in range(1, count) if counts[i] < limit]
        mass, left = sum([loads[i] for i in free]), rest
        for i in free:
            addition = min(limit - counts[i], max(1, left * loads[i] // mass), rest)
            counts[i] = counts[i] + addition
            rest = rest - addition
    return np.array(counts)


def noise(stream_key, dims, spread, reach, pieces=(), held_as=jnp.bfloat16):
    drawn = jax.random.normal(stream_key, dims, jnp.float32) * spread
    if len(pieces) > 0:
        drawn = shard_levels(stream_key, dims, pieces, -0.22, 0.18) * drawn
    return jnp.clip(drawn, min=-reach, max=reach).astype(held_as)


def setup_inputs(seed: int = 0) -> dict:
    streams_of = jax.random.split(jax.random.key(seed), 15)
    text_embed = noise(streams_of[0], (TOKENS, D), 1.0, 6.0, ((0, 32),))
    image_feats = noise(streams_of[1], (IMG_TOKENS, VIS), 1.0, 6.0, ((0, 32),))
    tile_pos = draw_tile_pos(jax.random.fold_in(streams_of[14], 71), 0)
    proj_in = noise(streams_of[3], (VIS, D), VIS ** -0.5, 0.09375, ((1, 4),))
    proj_out = noise(streams_of[4], (D, D), D ** -0.5, 0.125, ((0, 4),))
    norm_gain = jnp.clip(1.0 + 0.18 * jax.random.normal(streams_of[5], (D,), jnp.float32), 0.1, 1.9)
    shared_gate = noise(streams_of[6], (D, FFS), D ** -0.5, 0.125, ((1, 4),))
    shared_up = noise(streams_of[7], (D, FFS), D ** -0.5, 0.125, ((1, 4),))
    shared_down = noise(streams_of[8], (FFS, D), FFS ** -0.5, 0.109375, ((0, 4),))
    expert_gate = noise(streams_of[9], (EXPERTS, D, FF), D ** -0.5, 0.125, ((0, 8), (2, 4)))
    expert_up = noise(streams_of[10], (EXPERTS, D, FF), D ** -0.5, 0.125, ((0, 8), (2, 4)))
    expert_down = noise(streams_of[11], (EXPERTS, FF, D), FF ** -0.5, 0.15625, ((0, 8), (1, 4)))
    route_ids_keys = jax.random.split(jax.random.fold_in(streams_of[12], 1), TOKENS // GROUP_TOK)
    route_ids_turns = jax.random.permutation(jax.random.fold_in(streams_of[12], 3), TOKENS // GROUP_TOK)
    route_ids = jax.vmap(lambda own, number: routed_block(jax.random.fold_in(streams_of[12], 2), own, number, GROUP_TOK, EXPERTS, TOP, CAP, 2))(route_ids_keys, route_ids_turns).reshape((TOKENS, TOP))
    route_wts = plant(jax.random.randint(streams_of[13], (TOKENS, TOP), 1, 65536), jax.random.fold_in(streams_of[13], 1), 1, 65535).astype(jnp.int32)
    return {"text_embed": text_embed, "image_feats": image_feats, "tile_pos": tile_pos, "proj_in": proj_in, "proj_out": proj_out, "norm_gain": norm_gain, "shared_gate": shared_gate, "shared_up": shared_up, "shared_down": shared_down, "expert_gate": expert_gate, "expert_up": expert_up, "expert_down": expert_down, "route_ids": route_ids, "route_wts": route_wts}


def reference(text_embed, image_feats, tile_pos, proj_in, proj_out, norm_gain, shared_gate, shared_up, shared_down, expert_gate, expert_up, expert_down, route_ids, route_wts):
    vis_hidden = jax.nn.gelu(jnp.dot(image_feats, proj_in, preferred_element_type=jnp.float32), approximate=True).astype(jnp.bfloat16)
    projected = jnp.dot(vis_hidden, proj_out, preferred_element_type=jnp.float32).astype(jnp.bfloat16)
    embed = text_embed.at[tile_pos].set(projected)
    embed_f = embed.astype(jnp.float32)
    meansq = lax.optimization_barrier(jnp.mean(embed_f * embed_f, axis=-1, keepdims=True)) + 1e-06
    normed = (embed_f * lax.rsqrt(meansq) * norm_gain).astype(jnp.bfloat16)
    gate_s = jnp.dot(normed, shared_gate, preferred_element_type=jnp.float32)
    up_s = jnp.dot(normed, shared_up, preferred_element_type=jnp.float32)
    shared_hidden = (jax.nn.silu(gate_s) * up_s).astype(jnp.bfloat16)
    shared_out = jnp.dot(shared_hidden, shared_down, preferred_element_type=jnp.float32)
    weights_f = route_wts.astype(jnp.float32)
    weights_n = weights_f / lax.optimization_barrier(jnp.sum(weights_f, axis=-1, keepdims=True))
    ngroups = TOKENS // GROUP_TOK
    pairs = GROUP_TOK * TOP
    ids = route_ids.reshape(ngroups, pairs)
    onehot = (ids[:, :, None] == jnp.arange(EXPERTS, dtype=jnp.int32)[None, None, :]).astype(jnp.int32)
    rank = lax.optimization_barrier(jnp.sum(jnp.cumsum(onehot, axis=1) * onehot, axis=2)) - 1
    slot = ids * CAP + rank
    pair_index = jnp.broadcast_to(jnp.arange(pairs, dtype=jnp.int32)[None, :], (ngroups, pairs))
    group_index = jnp.broadcast_to(jnp.arange(ngroups, dtype=jnp.int32)[:, None], (ngroups, pairs))
    table = jnp.full((ngroups, EXPERTS * CAP), -1, dtype=jnp.int32)
    table = table.at[group_index, slot].set(pair_index)
    flat_weights = weights_n.reshape(ngroups, pairs)
    group_base = (jnp.arange(ngroups, dtype=jnp.int32) * GROUP_TOK)[:, None]
    fsplit = FF // N_EXPERT

    def one_expert(result, expert):
        source = lax.dynamic_slice_in_dim(table, expert * CAP, CAP, 1)
        valid = source >= 0
        safe = jnp.where(valid, source, 0).astype(jnp.int32)
        token = (safe // TOP + group_base).astype(jnp.int32)
        rows_in = jnp.where(valid[:, :, None], normed[token], jnp.zeros((), jnp.bfloat16)).astype(jnp.float32)
        gate_w = expert_gate[expert].astype(jnp.float32)
        up_w = expert_up[expert].astype(jnp.float32)
        down_w = expert_down[expert].astype(jnp.float32).reshape(N_EXPERT, fsplit, D)
        gate_e = jnp.einsum('gcd,df->gcf', rows_in, gate_w)
        up_e = jnp.einsum('gcd,df->gcf', rows_in, up_w)
        hidden_e = (jax.nn.silu(gate_e) * up_e).astype(jnp.bfloat16)
        hidden_e = hidden_e.astype(jnp.float32).reshape(ngroups, CAP, N_EXPERT, fsplit)
        partial_value = jnp.einsum('gcnf,nfd->gcnd', hidden_e, down_w)
        partial_value = lax.optimization_barrier(partial_value.astype(jnp.bfloat16))
        expert_out = lax.optimization_barrier(jnp.sum(partial_value.astype(jnp.float32), axis=2)).astype(jnp.bfloat16)
        coef = jnp.where(valid, jnp.take_along_axis(flat_weights, safe, axis=1), 0.0)
        result = result.at[token].add(coef[:, :, None] * expert_out.astype(jnp.float32))
        return (result, None)
    routed_out, _ = lax.scan(one_expert, jnp.zeros((TOKENS, D), jnp.float32), jnp.arange(EXPERTS, dtype=jnp.int32))
    return (embed_f + shared_out + routed_out).astype(jnp.bfloat16)
```

```python
import jax
import jax.numpy as jnp
from jax import lax
from jax.sharding import PartitionSpec as P

BF = jnp.bfloat16
F32 = jnp.float32


def dot(a, b):
    return jnp.dot(a, b, preferred_element_type=F32)


def swap(rows, axis, mask):
    count = lax.axis_size(axis)
    return lax.ppermute(rows, axis, [(i, i ^ mask) for i in range(count)])


def gather_blocks(block, axis):
    count = lax.axis_size(axis)
    me = lax.axis_index(axis)
    held = block[None]
    mask = count // 2
    while mask:
        other = swap(held, axis, mask)
        low = (me & mask) == 0
        first = jnp.where(low, held, other)
        second = jnp.where(low, other, held)
        held = jnp.stack([first, second], axis=1).reshape((-1,) + block.shape)
        mask //= 2
    return held


def scatter_sum(parts, axis):
    count = lax.axis_size(axis)
    me = lax.axis_index(axis)
    held = parts
    mask = 1
    while mask < count:
        pairs = held.reshape((held.shape[0] // 2, 2) + held.shape[1:])
        bit = (me // mask) & 1
        keep = lax.dynamic_index_in_dim(pairs, bit, 1, keepdims=False)
        give = lax.dynamic_index_in_dim(pairs, 1 - bit, 1, keepdims=False)
        held = (keep.astype(F32) + swap(give, axis, mask).astype(F32)).astype(BF)
        mask *= 2
    return held[0]


def one_hot(places, count):
    return places[None, :] == jnp.arange(count, dtype=jnp.int32)[:, None]


def shards(
    text_embed,
    image_feats,
    tile_pos,
    proj_in,
    proj_out,
    norm_gain,
    shared_gate,
    shared_up,
    shared_down,
    expert_gate,
    expert_up,
    expert_down,
    route_ids,
    route_wts,
):
    tok_dev, width = text_embed.shape
    img_dev = image_feats.shape[0]
    n_data = lax.axis_size("dp")
    n_group = lax.axis_size("expert")
    peer = img_dev // n_data
    my_place = lax.axis_index("expert")
    top = route_ids.shape[1]
    group_rows = tok_dev * n_group
    capacity = 3 * group_rows * top // (2 * n_data)
    share = capacity // n_group

    feats = gather_blocks(image_feats, "expert").reshape(n_group * img_dev, -1)
    vis_hidden = jax.nn.gelu(dot(feats, proj_in), approximate=True).astype(BF)
    part = dot(vis_hidden, proj_out).astype(BF)
    projected = scatter_sum(part.reshape(n_group, img_dev, width), "expert")

    owner = tile_pos // tok_dev // n_group
    earlier = jnp.arange(img_dev)[None, :] < jnp.arange(img_dev)[:, None]
    rank_img = jnp.sum(((owner[:, None] == owner[None, :]) & earlier).astype(jnp.int32), axis=1)
    place = one_hot(owner * peer + rank_img, img_dev).astype(BF)
    offsets = jnp.broadcast_to((tile_pos % tok_dev).astype(BF)[:, None], (img_dev, 128))
    leaving = dot(place, jnp.concatenate([projected, offsets], axis=1)).astype(BF)
    arrived = lax.all_to_all(
        leaving.reshape(n_data, peer, width + 128), "dp", split_axis=0, concat_axis=0, tiled=True
    ).reshape(img_dev, width + 128)
    spots = one_hot(arrived[:, width].astype(jnp.int32), tok_dev)
    image_rows = dot(spots.astype(BF), arrived[:, :width]).astype(BF)
    embed = jnp.where(jnp.any(spots, axis=1, keepdims=True), image_rows, text_embed)

    embed_f = embed.astype(F32)
    meansq = jnp.mean(embed_f * embed_f, axis=-1, keepdims=True) + 1e-06
    normed_own = (embed_f * lax.rsqrt(meansq) * norm_gain).astype(BF)
    normed = gather_blocks(normed_own, "expert").reshape(group_rows, width)

    routes = gather_blocks(jnp.concatenate([route_ids, route_wts], axis=1), "expert")
    routes = routes.reshape(group_rows, 2 * top)
    ids, weights = routes[:, :top], routes[:, top:].astype(F32)
    weights = weights / jnp.sum(weights, axis=1, keepdims=True)
    named = ids[:, :, None] == jnp.arange(n_data, dtype=jnp.int32)[None, None, :]
    before = jnp.arange(group_rows)[None, :] < jnp.arange(group_rows)[:, None]
    counts = dot(before.astype(BF), jnp.any(named, axis=1).astype(BF))
    rank = jnp.sum(jnp.where(named, counts[:, None, :], 0.0), axis=2).astype(jnp.int32)
    slot = jnp.where(rank // share == my_place, ids * share + rank % share, -1)
    hits = [one_hot(slot[:, k], n_data * share) for k in range(top)]
    picks = sum(hit.astype(BF) for hit in hits)
    coef = sum(jnp.where(hit, weights[:, k][None, :], 0.0) for k, hit in enumerate(hits))

    send = dot(picks, normed).astype(BF).reshape(n_data, share, width)
    slots = lax.all_to_all(send, "dp", split_axis=0, concat_axis=0, tiled=True)
    rows = gather_blocks(slots.reshape(n_data * share, width), "expert").reshape(-1, width)
    gate_e, up_e = dot(rows, expert_gate[0]), dot(rows, expert_up[0])
    hidden_e = (jax.nn.silu(gate_e) * up_e).astype(BF)
    part_e = dot(hidden_e, expert_down[0]).astype(BF)
    summed = scatter_sum(part_e.reshape(n_group, n_data * share, width), "expert")
    returned = lax.all_to_all(
        summed.reshape(n_data, share, width), "dp", split_axis=0, concat_axis=0, tiled=True
    ).reshape(n_data * share, width)

    gate_s, up_s = dot(normed, shared_gate), dot(normed, shared_up)
    shared_hidden = (jax.nn.silu(gate_s) * up_s).astype(BF)
    coef_hi = coef.astype(BF)
    coef_lo = (coef - coef_hi.astype(F32)).astype(BF)
    total = dot(shared_hidden, shared_down) + dot(coef_hi.T, returned) + dot(coef_lo.T, returned)
    total = scatter_sum(total.astype(BF).reshape(n_group, tok_dev, width), "expert")
    return (embed_f + total.astype(F32)).astype(BF)


def solution(mesh):
    return jax.shard_map(
        shards,
        mesh=mesh,
        in_specs=(
            P(("dp", "expert"), None),
            P(("dp", "expert"), None),
            P(("dp", "expert")),
            P(None, "expert"),
            P("expert", None),
            P(),
            P(None, "expert"),
            P(None, "expert"),
            P("expert", None),
            P("dp", None, "expert"),
            P("dp", None, "expert"),
            P("dp", "expert", None),
            P(("dp", "expert"), None),
            P(("dp", "expert"), None),
        ),
        out_specs=P(("dp", "expert"), None),
        check_vma=False,
    )
```

```python
import jax
import jax.numpy as jnp
from jax import lax
from jax.experimental import pallas as pl
from jax.experimental.pallas import tpu as pltpu
from jax.sharding import PartitionSpec as P

BF = jnp.bfloat16
F32 = jnp.float32


def dot(a, b):
    return jnp.dot(a, b, preferred_element_type=F32)


def dot_t(a, b):
    return lax.dot_general(a, b, (((1,), (1,)), ((), ())), preferred_element_type=F32)


def swap(rows, axis, mask):
    count = lax.axis_size(axis)
    return lax.ppermute(rows, axis, [(i, i ^ mask) for i in range(count)])


def gather(piece, axis):
    mask = lax.axis_size(axis) // 2
    pieces = [piece]
    while mask:
        pieces = pieces + [swap(p, axis, mask) for p in pieces]
        mask //= 2
    return pieces


def add(rows, other):
    return (rows.astype(F32) + other.astype(F32)).astype(BF)


def scatter_sum(keep, give, axis, last=None):
    rows, mask = add(keep, swap(give, axis, 1)), 2
    while mask < (last or lax.axis_size(axis)):
        half = rows.shape[0] // 2
        rows = add(rows[:half], swap(rows[half:], axis, mask))
        mask *= 2
    return rows


def reversed_bits(places, count):
    turned, mask, low = jnp.zeros_like(places), count // 2, 1
    while mask:
        turned += jnp.where((places & low) != 0, mask, 0)
        mask, low = mask // 2, low * 2
    return turned


def local_kernel(body, outs, args, scratch=(), macs=0):
    moved = sum(x.size * x.dtype.itemsize for x in args) + sum(
        o.size * o.dtype.itemsize for o in outs
    )
    return pl.pallas_call(
        body,
        out_shape=list(outs),
        in_specs=[pl.BlockSpec(memory_space=pltpu.VMEM)] * len(args),
        out_specs=[pl.BlockSpec(memory_space=pltpu.VMEM)] * len(outs),
        scratch_shapes=list(scratch),
        compiler_params=pltpu.CompilerParams(vmem_limit_bytes=48 * 2**20),
        cost_estimate=pl.CostEstimate(flops=2 * macs, bytes_accessed=moved, transcendentals=0),
    )(*args)


def put_together(refs, whole):
    at = 0
    for ref in refs:
        whole[at : at + ref.shape[0]] = ref[...]
        at += ref.shape[0]


def out(rows, columns, dtype=BF):
    return jax.ShapeDtypeStruct((rows, columns), dtype)


def steps_of(size, step):
    return size // step if size % step == 0 else 1


def gated(rows, gate, up):
    value = dot_t(rows, gate)
    return (value / (1.0 + jnp.exp(-value)) * dot_t(rows, up)).astype(BF)


def fits(pieces):
    return all(p.shape[0] % 16 == 0 for p in pieces)


def expert_rows(pieces, gate, up, down):
    count = sum(p.shape[0] for p in pieces)
    units, width = gate.shape
    if not fits(pieces) or count % 32:
        part = dot(gated(jnp.concatenate(pieces, axis=0), gate, up), down).astype(BF)
        return part[: count // 2], part[count // 2 :]

    def body(*refs):
        n = len(pieces)
        gate_ref, up_ref, down_ref, keep, give, whole = refs[n:]
        put_together(refs[:n], whole)
        for rows, result in ((slice(count // 2, count), give), (slice(0, count // 2), keep)):
            hidden = gated(whole[rows], gate_ref[...], up_ref[...])
            result[...] = dot(hidden, down_ref[...]).astype(BF)

    return local_kernel(
        body,
        [out(count // 2, width)] * 2,
        [*pieces, gate, up, down],
        [pltpu.VMEM((count, width), BF)],
        3 * count * width * units,
    )


def shared_rows(pieces, gate, up, down):
    count = sum(p.shape[0] for p in pieces)
    units, width = gate.shape
    if not fits(pieces):
        part = dot(gated(jnp.concatenate(pieces, axis=0), gate, up), down)
        return part[: count // 2], part[count // 2 :]

    def body(*refs):
        n = len(pieces)
        gate_ref, up_ref, down_ref, keep, give, whole = refs[n:]
        put_together(refs[:n], whole)
        part = dot(gated(whole[...], gate_ref[...], up_ref[...]), down_ref[...])
        keep[...] = part[: count // 2]
        give[...] = part[count // 2 :]

    return local_kernel(
        body,
        [out(count // 2, width, F32)] * 2,
        [*pieces, gate, up, down],
        [pltpu.VMEM((count, width), BF)],
        3 * count * width * units,
    )


def image_rows(pieces, proj_in, proj_out):
    count = sum(p.shape[0] for p in pieces)
    depth, units = proj_in.shape
    width = proj_out.shape[1]

    def body(*refs):
        n = len(pieces)
        in_ref, out_ref, keep, give, whole = refs[n:]
        put_together(refs[:n], whole)
        hidden = jax.nn.gelu(dot(whole[...], in_ref[...]), approximate=True).astype(BF)
        part = dot(hidden, out_ref[...])
        keep[...] = part[: count // 2].astype(BF)
        give[...] = part[count // 2 :].astype(BF)

    return local_kernel(
        body,
        [out(count // 2, width)] * 2,
        [*pieces, proj_in, proj_out],
        [pltpu.VMEM((count, depth), BF)],
        count * units * (depth + width),
    )


def place_rows(mine, other, place, offsets, n_data):
    count, width = mine.shape
    peer = count // n_data
    wide = width + offsets.shape[1]
    if count % 16:
        rows = jnp.concatenate([add(mine, other), offsets], axis=1)
        return dot(place, rows).astype(BF).reshape(n_data, peer, wide)

    def body(mine_ref, other_ref, place_ref, offsets_ref, result):
        rows = add(mine_ref[...], other_ref[...])
        moved = dot(place_ref[...], rows).astype(BF)
        beside = dot(place_ref[...], offsets_ref[...]).astype(BF)
        for d in range(n_data):
            result[d, :, :width] = moved[d * peer : (d + 1) * peer]
            result[d, :, width:] = beside[d * peer : (d + 1) * peer]

    return local_kernel(
        body,
        [jax.ShapeDtypeStruct((n_data, peer, wide), BF)],
        [mine, other, place, offsets],
        (),
        count * count * wide,
    )[0]


def embed_rows(arrived, text, gain):
    n_data, peer, wide = arrived.shape
    count, width = text.shape

    def math(rows, offsets, text_rows, gain_row):
        spots = lax.broadcasted_iota(jnp.int32, (1, count), 1).astype(F32) == offsets
        spots = spots.astype(F32)
        turned = (((0,), (0,)), ((), ()))
        placed = lax.dot_general(spots.astype(BF), rows, turned, preferred_element_type=F32)
        named = lax.dot_general(spots, jnp.ones_like(offsets), turned, preferred_element_type=F32)
        embed = jnp.where(named > 0.5, placed, text_rows.astype(F32))
        meansq = jnp.mean(embed * embed, axis=-1, keepdims=True) + 1e-06
        return embed, (embed * lax.rsqrt(meansq) * gain_row).astype(BF)

    gain = gain.reshape(1, width)
    if n_data * peer % 16 or peer % 4:
        rows = arrived.reshape(n_data * peer, wide)
        return math(rows[:, :width], rows[:, width : width + 1].astype(F32), text, gain)

    def body(arrived_ref, text_ref, gain_ref, embed_ref, normed_ref):
        rows = jnp.concatenate([arrived_ref[d].astype(F32) for d in range(n_data)], axis=0)
        embed, normed = math(
            rows[:, :width].astype(BF), rows[:, width : width + 1], text_ref[...], gain_ref[...]
        )
        embed_ref[...] = embed
        normed_ref[...] = normed

    return local_kernel(
        body, [out(count, width, F32), out(count, width)], [arrived, text, gain], (), count * n_data * peer * width
    )


def pick_rows(picks, pieces, starts, sizes):
    count, width = sum(p.shape[0] for p in pieces), pieces[0].shape[1]
    if not fits(pieces) or any(n % 8 for n in (*starts, *sizes)):
        rows = dot(picks, jnp.concatenate(pieces, axis=0)).astype(BF)
        return [rows[at : at + size] for at, size in zip(starts, sizes)]

    def body(*refs):
        n = len(pieces)
        whole = refs[-1]
        put_together(refs[1 : n + 1], whole)
        rows = dot(refs[0][...], whole[...])
        for ref, at, size in zip(refs[n + 1 : -1], starts, sizes):
            ref[...] = rows[at : at + size].astype(BF)

    return local_kernel(
        body,
        [out(size, width) for size in sizes],
        [picks, *pieces],
        [pltpu.VMEM((count, width), BF)],
        picks.shape[0] * count * width,
    )


def combine_rows(total, coef, backs, starts):
    count, width = total.shape
    slots = coef.shape[2]
    ends = list(starts[1:]) + [slots]
    if any(n % 16 for n in (slots, *starts)):
        whole = jnp.concatenate(
            [jnp.pad(b, ((0, e - s - b.shape[0]), (0, 0))) for b, s, e in zip(backs, starts, ends)],
            axis=0,
        )
        return (total + dot(coef[0], whole) + dot(coef[1], whole)).astype(BF)

    def body(*refs):
        total_ref, coef_ref, result, whole = refs[0], refs[1], refs[-2], refs[-1]
        for ref, at, end in zip(refs[2:-2], starts, ends):
            size = ref.shape[0]
            if size != end - at:
                whole[end - 16 : end] = jnp.zeros((16, width), BF)
            whole[at : at + size] = ref[...]
        rows = whole[...]
        value = total_ref[...] + dot(coef_ref[0], rows)
        result[...] = (value + dot(coef_ref[1], rows)).astype(BF)

    return local_kernel(
        body,
        [out(count, width)],
        [total, coef, *backs],
        [pltpu.VMEM((slots, width), BF)],
        2 * count * width * slots,
    )[0]


def one_hot(places, count):
    return places[None, :] == jnp.arange(count, dtype=jnp.int32)[:, None]


def shards(
    text_embed,
    image_feats,
    tile_pos,
    proj_in,
    proj_out,
    norm_gain,
    shared_gate,
    shared_up,
    shared_down,
    expert_gate,
    expert_up,
    expert_down,
    route_ids,
    route_wts,
):
    tok_dev, width = text_embed.shape
    img_dev = image_feats.shape[0]
    n_data = lax.axis_size("dp")
    n_group = lax.axis_size("expert")
    peer = img_dev // n_data
    my_place = lax.axis_index("expert")
    top = route_ids.shape[1]
    group_rows = tok_dev * n_group
    capacity = 3 * group_rows * top // (2 * n_data)
    share = capacity // n_group

    keep, give = image_rows(gather(image_feats, "expert"), proj_in, proj_out)
    rows, mask = add(keep, swap(give, "expert", 1)), 2
    while 2 * mask < n_group:
        half = rows.shape[0] // 2
        rows = add(rows[:half], swap(rows[half:], "expert", mask))
        mask *= 2
    other = swap(rows[img_dev:], "expert", mask)

    owner = tile_pos // tok_dev // n_group
    earlier = jnp.arange(img_dev)[None, :] < jnp.arange(img_dev)[:, None]
    rank_img = jnp.sum(((owner[:, None] == owner[None, :]) & earlier).astype(jnp.int32), axis=1)
    place = one_hot(owner * peer + rank_img, img_dev).astype(BF)
    offsets = jnp.broadcast_to((tile_pos % tok_dev).astype(BF)[:, None], (img_dev, 128))
    leaving = place_rows(rows[:img_dev], other, place, offsets, n_data)
    arrived = lax.all_to_all(leaving, "dp", split_axis=0, concat_axis=0, tiled=True)
    embed_f, normed = embed_rows(arrived, text_embed, norm_gain)
    normed = gather(normed, "expert")

    routes = jnp.concatenate([route_ids, route_wts], axis=1)
    routes = jnp.concatenate(gather(routes, "expert"), axis=0)
    ids, weights = routes[:, :top], routes[:, top:].astype(F32)
    weights = weights / jnp.sum(weights, axis=1, keepdims=True)
    rows_at = jnp.arange(group_rows, dtype=jnp.int32)
    token = (my_place ^ reversed_bits(rows_at // tok_dev, n_group)) * tok_dev + rows_at % tok_dev
    named = ids[:, :, None] == jnp.arange(n_data, dtype=jnp.int32)[None, None, :]
    before = token[None, :] < token[:, None]
    counts = dot(before.astype(BF), jnp.any(named, axis=1).astype(BF))
    rank = jnp.sum(jnp.where(named, counts[:, None, :], 0.0), axis=2).astype(jnp.int32)
    distance = ids ^ lax.axis_index("dp")

    half = n_data // 2
    wide = 2 * capacity // 4
    core = my_place % 2
    near_slot = jnp.where((distance < half) & (rank // wide == core), distance * wide + rank % wide, -1)
    apart = -(-share // 16) * 16
    far_slot = jnp.where(
        (distance >= half) & (rank // share == my_place),
        (distance - half) * apart + rank % share + half * wide,
        -1,
    )
    slot = jnp.maximum(near_slot, far_slot)
    sizes = [wide] * half + [share] * (n_data - half)
    starts = [m * wide if m < half else half * wide + (m - half) * apart for m in range(n_data)]
    slots = half * wide + (n_data - half) * apart
    hits = [one_hot(slot[:, k], slots) for k in range(top)]
    picks = sum(hit.astype(BF) for hit in hits)
    coef = sum(jnp.where(hit, weights[:, k][None, :], 0.0) for k, hit in enumerate(hits)).T
    coef_hi = coef.astype(BF)
    coef = jnp.stack([coef_hi, (coef - coef_hi.astype(F32)).astype(BF)])

    send = pick_rows(picks, normed, starts, sizes)
    got = [None] * n_data
    got[0] = send[0]
    quarter = n_data // 4
    near, far_one, far_two = range(half), range(half, half + quarter), range(half + quarter, n_data)
    for m in (*near[1:], *far_one):
        got[m] = swap(send[m], "dp", m)
    for i, m in enumerate(far_two):
        late, got[i + 1] = lax.optimization_barrier((send[m], got[i + 1]))
        got[m] = swap(late, "dp", m)

    shared = shared_rows(normed, shared_gate.T, shared_up.T, shared_down)
    experts = (expert_gate[0].T, expert_up[0].T, expert_down[0])

    def join(stage):
        return jnp.concatenate([got[m] for m in stage], axis=0)

    far = join(far_one)
    far, shared = lax.optimization_barrier((far, shared))
    far_pieces = gather(far, "expert")
    mine = [got[m] for m in near]
    keep, give = expert_rows(mine + [swap(p, "expert", 1) for p in mine], *experts)
    far_pieces, keep, give = lax.optimization_barrier((far_pieces, keep, give))
    back = [None] * n_data

    def send_back(stage, rows):
        size = sizes[stage[0]]
        for i, m in enumerate(stage):
            part = rows[i * size : (i + 1) * size]
            back[m] = swap(part, "dp", m) if m else part

    send_back(near, scatter_sum(keep, give, "expert", last=2))
    send_back(far_one, scatter_sum(*expert_rows(far_pieces, *experts), "expert"))
    pieces = gather(join(far_two), "expert")
    send_back(far_two, scatter_sum(*expert_rows(pieces, *experts), "expert"))

    middle = group_rows // 2
    give = combine_rows(shared[1], coef[:, middle:], back, starts)
    keep = combine_rows(shared[0], coef[:, :middle], back, starts)
    total = scatter_sum(keep, give, "expert")
    return (embed_f + total.astype(F32)).astype(BF)


def solution(mesh):
    return jax.shard_map(
        shards,
        mesh=mesh,
        in_specs=(
            P(("dp", "expert"), None),
            P(("dp", "expert"), None),
            P(("dp", "expert")),
            P(None, "expert"),
            P("expert", None),
            P(),
            P(None, "expert"),
            P(None, "expert"),
            P("expert", None),
            P("dp", None, "expert"),
            P("dp", None, "expert"),
            P("dp", "expert", None),
            P(("dp", "expert"), None),
            P(("dp", "expert"), None),
        ),
        out_specs=P(("dp", "expert"), None),
        check_vma=False,
    )
```

```python
import jax
import jax.numpy as jnp
from jax import lax
from jax.experimental import pallas as pl
from jax.experimental.pallas import tpu as pltpu
from jax.sharding import PartitionSpec as P

BF = jnp.bfloat16
F32 = jnp.float32


def dot(a, b):
    return jnp.dot(a, b, preferred_element_type=F32)


def dot_t(a, b):
    return lax.dot_general(a, b, (((1,), (1,)), ((), ())), preferred_element_type=F32)


def swap(rows, axis, mask):
    count = lax.axis_size(axis)
    return lax.ppermute(rows, axis, [(i, i ^ mask) for i in range(count)])


def gather(piece, axis):
    mask = lax.axis_size(axis) // 2
    pieces = [piece]
    while mask:
        pieces = pieces + [swap(p, axis, mask) for p in pieces]
        mask //= 2
    return pieces


def spread(piece):
    mask = lax.axis_size("expert") // 2
    pieces = [piece]
    while mask > 1:
        pieces = pieces + [swap(p, "expert", mask) for p in pieces]
        mask //= 2
    return pieces


def add(rows, other):
    return (rows.astype(F32) + other.astype(F32)).astype(BF)


def sum_rest(rows):
    mask = 2
    while mask < lax.axis_size("expert"):
        half = rows.shape[0] // 2
        rows = add(rows[:half], swap(rows[half:], "expert", mask))
        mask *= 2
    return rows


def reversed_bits(places, count):
    turned, mask, low = jnp.zeros_like(places), count // 2, 1
    while mask:
        turned += jnp.where((places & low) != 0, mask, 0)
        mask, low = mask // 2, low * 2
    return turned


def local_kernel(body, outs, args, scratch=(), macs=0):
    moved = sum(x.size * x.dtype.itemsize for x in args) + sum(
        o.size * o.dtype.itemsize for o in outs
    )
    return pl.pallas_call(
        body,
        out_shape=list(outs),
        in_specs=[pl.BlockSpec(memory_space=pltpu.VMEM)] * len(args),
        out_specs=[pl.BlockSpec(memory_space=pltpu.VMEM)] * len(outs),
        scratch_shapes=list(scratch),
        compiler_params=pltpu.CompilerParams(vmem_limit_bytes=12 * 2**20),
        cost_estimate=pl.CostEstimate(flops=2 * macs, bytes_accessed=moved, transcendentals=0),
    )(*args)


def fetch(*arrays):
    def body(*refs):
        n = len(arrays)
        sems = refs[-1]
        copies = [pltpu.make_async_copy(refs[i], refs[n + i], sems.at[i]) for i in range(n)]
        for copy in copies:
            copy.start()
        for copy in copies:
            copy.wait()

    return pl.pallas_call(
        body,
        out_shape=[jax.ShapeDtypeStruct(x.shape, x.dtype) for x in arrays],
        in_specs=[pl.BlockSpec(memory_space=pltpu.HBM)] * len(arrays),
        out_specs=[pl.BlockSpec(memory_space=pltpu.VMEM)] * len(arrays),
        scratch_shapes=[pltpu.SemaphoreType.DMA((len(arrays),))],
        compiler_params=pltpu.CompilerParams(vmem_limit_bytes=2**20),
    )(*arrays)


def fence(*values):
    return lax.optimization_barrier(values)


def put_together(refs, whole):
    at = 0
    for ref in refs:
        whole[at : at + ref.shape[0]] = ref[...]
        at += ref.shape[0]


def out(rows, columns, dtype=BF):
    return jax.ShapeDtypeStruct((rows, columns), dtype)


def steps_of(size, step):
    return size // step if size % step == 0 else 1


def gated(rows, gate, up):
    value = dot_t(rows, gate)
    return (value / (1.0 + jnp.exp(-value)) * dot_t(rows, up)).astype(BF)


def fits(pieces):
    return all(p.shape[0] % 16 == 0 for p in pieces)


def expert_rows(pieces, gate, up, down):
    count = sum(p.shape[0] for p in pieces)
    units, width = gate.shape
    if not fits(pieces) or count % 32:
        part = dot(gated(jnp.concatenate(pieces, axis=0), gate, up), down).astype(BF)
        return part[: count // 2], part[count // 2 :]

    def body(*refs):
        n = len(pieces)
        gate_ref, up_ref, down_ref, keep, give, whole = refs[n:]
        put_together(refs[:n], whole)
        if count <= 256:
            part = dot(gated(whole[...], gate_ref[...], up_ref[...]), down_ref[...])
            keep[...] = part[: count // 2].astype(BF)
            give[...] = part[count // 2 :].astype(BF)
            return
        for rows, result in ((slice(count // 2, count), give), (slice(0, count // 2), keep)):
            hidden = gated(whole[rows], gate_ref[...], up_ref[...])
            result[...] = dot(hidden, down_ref[...]).astype(BF)

    return local_kernel(
        body,
        [out(count // 2, width)] * 2,
        [*pieces, gate, up, down],
        [pltpu.VMEM((count, width), BF)],
        3 * count * width * units,
    )


def shared_rows(pieces, gate, up, down):
    count = sum(p.shape[0] for p in pieces)
    units, width = gate.shape
    if not fits(pieces):
        part = dot(gated(jnp.concatenate(pieces, axis=0), gate, up), down)
        return part[: count // 2], part[count // 2 :]

    def body(*refs):
        n = len(pieces)
        gate_ref, up_ref, down_ref, keep, give, whole = refs[n:]
        put_together(refs[:n], whole)
        part = dot(gated(whole[...], gate_ref[...], up_ref[...]), down_ref[...])
        keep[...] = part[: count // 2]
        give[...] = part[count // 2 :]

    return local_kernel(
        body,
        [out(count // 2, width, F32)] * 2,
        [*pieces, gate, up, down],
        [pltpu.VMEM((count, width), BF)],
        3 * count * width * units,
    )


def image_rows(pieces, proj_in, proj_out):
    count = sum(p.shape[0] for p in pieces)
    depth, units = proj_in.shape
    width = proj_out.shape[1]

    def body(*refs):
        n = len(pieces)
        in_ref, out_ref, keep, give, whole = refs[n:]
        put_together(refs[:n], whole)
        hidden = jax.nn.gelu(dot(whole[...], in_ref[...]), approximate=True).astype(BF)
        part = dot(hidden, out_ref[...])
        keep[...] = part[: count // 2].astype(BF)
        give[...] = part[count // 2 :].astype(BF)

    return local_kernel(
        body,
        [out(count // 2, width)] * 2,
        [*pieces, proj_in, proj_out],
        [pltpu.VMEM((count, depth), BF)],
        count * units * (depth + width),
    )


def place_rows(mine, other, place, offsets, n_data):
    count, width = mine.shape
    blocks, size = place.shape[:2]
    peer = size // n_data
    wide = width + offsets.shape[1]
    if size % 16:
        rows = jnp.concatenate([add(mine, other), offsets], axis=1).reshape(blocks, size, wide)
        moved = jnp.einsum("bsr,brw->bsw", place, rows, preferred_element_type=F32).astype(BF)
        return moved.reshape(blocks, n_data, peer, wide).swapaxes(0, 1).reshape(n_data, -1, wide)

    def body(mine_ref, other_ref, place_ref, offsets_ref, result):
        moved, beside = [], []
        for b in range(blocks):
            span = slice(b * size, (b + 1) * size)
            moved.append(dot(place_ref[b], add(mine_ref[span], other_ref[span])))
            beside.append(dot(place_ref[b], offsets_ref[span]))
        for d in range(n_data):
            part = slice(d * peer, (d + 1) * peer)
            result[d, :, :width] = jnp.concatenate([m[part] for m in moved], axis=0).astype(BF)
            result[d, :, width:] = jnp.concatenate([m[part] for m in beside], axis=0).astype(BF)

    return local_kernel(
        body,
        [jax.ShapeDtypeStruct((n_data, blocks * peer, wide), BF)],
        [mine, other, place, offsets],
        (),
        count * size * wide,
    )[0]


def embed_rows(pieces, texts, gain, peer):
    n_data, stack, wide = pieces[0].shape
    count, width = texts[0].shape
    blocks = len(texts)
    total_rows, total = n_data * stack, blocks * count

    def in_order(piece, p):
        order = [p ^ b for b in range(blocks)]
        return piece if p == 0 else jnp.concatenate([piece[o * peer : (o + 1) * peer] for o in order], axis=0)

    def math(parts, text, gain_row):
        rows = parts[0][:, :width]
        for part in parts[1:]:
            rows = rows + part[:, :width]
        line = lax.broadcasted_iota(jnp.int32, (total_rows, 1), 0)
        target = parts[0][:, width : width + 1] + (line // peer % blocks * count).astype(F32)
        spots = lax.broadcasted_iota(jnp.int32, (1, total), 1).astype(F32) == target
        spots = spots.astype(F32)
        turned = (((0,), (0,)), ((), ()))
        placed = lax.dot_general(spots.astype(BF), rows.astype(BF), turned, preferred_element_type=F32)
        named = lax.dot_general(spots, jnp.ones_like(target), turned, preferred_element_type=F32)
        embed = jnp.where(named > 0.5, placed, text.astype(F32))
        meansq = jnp.mean(embed * embed, axis=-1, keepdims=True) + 1e-06
        return embed[:count], (embed * lax.rsqrt(meansq) * gain_row).astype(BF)

    gain = gain.reshape(1, width)
    if stack % 8:
        parts = [
            jnp.concatenate([in_order(piece[d], p) for d in range(n_data)], axis=0).astype(F32)
            for p, piece in enumerate(pieces)
        ]
        return math(parts, jnp.concatenate(texts, axis=0), gain)

    def body(*refs):
        gain_ref, embed_ref, normed_ref = refs[2 * blocks :]
        parts = [
            jnp.concatenate([in_order(ref[d].astype(F32), p) for d in range(n_data)], axis=0)
            for p, ref in enumerate(refs[:blocks])
        ]
        text = jnp.concatenate([ref[...].astype(F32) for ref in refs[blocks : 2 * blocks]], axis=0)
        embed_ref[...], normed_ref[...] = math(parts, text, gain_ref[...])

    return local_kernel(
        body,
        [out(count, width, F32), out(total, width)],
        [*pieces, *texts, gain],
        (),
        total * total_rows * width,
    )


def pick_rows(picks, pieces, starts, sizes):
    count, width = sum(p.shape[0] for p in pieces), pieces[0].shape[1]
    if not fits(pieces) or any(n % 8 for n in (*starts, *sizes)):
        rows = dot(picks, jnp.concatenate(pieces, axis=0)).astype(BF)
        return [rows[at : at + size] for at, size in zip(starts, sizes)]

    def body(*refs):
        n = len(pieces)
        whole = refs[-1]
        put_together(refs[1 : n + 1], whole)
        rows = dot(refs[0][...], whole[...])
        for ref, at, size in zip(refs[n + 1 : -1], starts, sizes):
            ref[...] = rows[at : at + size].astype(BF)

    return local_kernel(
        body,
        [out(size, width) for size in sizes],
        [picks, *pieces],
        [pltpu.VMEM((count, width), BF)],
        picks.shape[0] * count * width,
    )


def combine_rows(total, coef, backs, starts, dtype):
    count, width = total.shape
    slots = coef.shape[2]
    ends = list(starts[1:]) + [slots]
    if any(n % 16 for n in (slots, *starts)):
        whole = jnp.concatenate(
            [jnp.pad(b, ((0, e - s - b.shape[0]), (0, 0))) for b, s, e in zip(backs, starts, ends)],
            axis=0,
        )
        return (total + dot(coef[0], whole) + dot(coef[1], whole)).astype(dtype)

    def body(*refs):
        total_ref, coef_ref, result, whole = refs[0], refs[1], refs[-2], refs[-1]
        for ref, at, end in zip(refs[2:-2], starts, ends):
            size = ref.shape[0]
            if size != end - at:
                whole[end - 16 : end] = jnp.zeros((16, width), BF)
            whole[at : at + size] = ref[...]
        rows = whole[...]
        value = total_ref[...] + dot(coef_ref[0], rows)
        result[...] = (value + dot(coef_ref[1], rows)).astype(dtype)

    return local_kernel(
        body,
        [out(count, width, dtype)],
        [total, coef, *backs],
        [pltpu.VMEM((slots, width), BF)],
        2 * count * width * slots,
    )[0]


def one_hot(places, count):
    return places[None, :] == jnp.arange(count, dtype=jnp.int32)[:, None]


def shards(
    text_embed,
    image_feats,
    tile_pos,
    proj_in,
    proj_out,
    norm_gain,
    shared_gate,
    shared_up,
    shared_down,
    expert_gate,
    expert_up,
    expert_down,
    route_ids,
    route_wts,
):
    tok_dev, width = text_embed.shape
    img_dev = image_feats.shape[0]
    n_data = lax.axis_size("dp")
    n_group = lax.axis_size("expert")
    peer = img_dev // n_data
    my_place = lax.axis_index("expert")
    top = route_ids.shape[1]
    group_rows = tok_dev * n_group
    capacity = 3 * group_rows * top // (2 * n_data)
    share = capacity // n_group

    weights_in, weights_out, own_feats = fetch(proj_in, proj_out, image_feats)
    routes = spread(jnp.concatenate([route_ids, route_wts], axis=1))
    spots, feats = spread(tile_pos), spread(image_feats)
    partner = [swap(image_feats, "expert", 1)]
    feats, partner, spots, routes, own_feats = fence(feats, partner, spots, routes, own_feats)
    feats = feats + partner + [swap(p, "expert", 1) for p in feats[1:]]
    keep, give = image_rows([own_feats, *feats[1:]], weights_in, weights_out)

    spots, keep, give = fence(spots, keep, give)
    spots = jnp.stack(spots)
    owner = spots // tok_dev // n_group
    earlier = jnp.arange(img_dev)[None, :] < jnp.arange(img_dev)[:, None]
    rank_img = jnp.sum(((owner[:, :, None] == owner[:, None, :]) & earlier).astype(jnp.int32), axis=2)
    seat = owner * peer + rank_img
    place = (seat[:, None, :] == jnp.arange(img_dev, dtype=jnp.int32)[None, :, None]).astype(BF)
    offsets = jnp.broadcast_to((spots % tok_dev).astype(BF).reshape(-1, 1), (spots.size, 128))
    leaving = place_rows(keep, swap(give, "expert", 1), place, offsets, n_data)
    texts, routes, leaving = fence(text_embed, routes, leaving)
    texts = spread(texts)
    routes = routes + [swap(p, "expert", 1) for p in routes]
    arrived = lax.all_to_all(leaving, "dp", split_axis=0, concat_axis=0, tiled=True)
    texts, routes, arrived = fence(texts, routes, arrived)
    embed_f, normed = embed_rows(spread(arrived), texts, norm_gain, peer)
    normed = [normed, swap(normed, "expert", 1)]

    routes = jnp.concatenate(routes, axis=0)
    ids, weights = routes[:, :top], routes[:, top:].astype(F32)
    weights = weights / jnp.sum(weights, axis=1, keepdims=True)
    rows_at = jnp.arange(group_rows, dtype=jnp.int32)
    token = (my_place ^ reversed_bits(rows_at // tok_dev, n_group)) * tok_dev + rows_at % tok_dev
    named = ids[:, :, None] == jnp.arange(n_data, dtype=jnp.int32)[None, None, :]
    before = token[None, :] < token[:, None]
    counts = dot(before.astype(BF), jnp.any(named, axis=1).astype(BF))
    rank = jnp.sum(jnp.where(named, counts[:, None, :], 0.0), axis=2).astype(jnp.int32)
    distance = ids ^ lax.axis_index("dp")

    half = n_data // 2
    wide = 2 * capacity // 4
    core = my_place % 2
    near_slot = jnp.where((distance < half) & (rank // wide == core), distance * wide + rank % wide, -1)
    apart = -(-share // 16) * 16
    far_slot = jnp.where(
        (distance >= half) & (rank // share == my_place),
        (distance - half) * apart + rank % share + half * wide,
        -1,
    )
    slot = jnp.maximum(near_slot, far_slot)
    sizes = [wide] * half + [share] * (n_data - half)
    starts = [m * wide if m < half else half * wide + (m - half) * apart for m in range(n_data)]
    slots = half * wide + (n_data - half) * apart
    hits = [one_hot(slot[:, k], slots) for k in range(top)]
    picks = sum(hit.astype(BF) for hit in hits)
    coef = sum(jnp.where(hit, weights[:, k][None, :], 0.0) for k, hit in enumerate(hits)).T
    coef_hi = coef.astype(BF)
    coef = jnp.stack([coef_hi, (coef - coef_hi.astype(F32)).astype(BF)])

    send = pick_rows(picks, normed, starts, sizes)
    got = [None] * n_data
    got[0] = send[0]
    quarter = n_data // 4
    near, far_one, far_two = range(half), range(half, half + quarter), range(half + quarter, n_data)
    for m in (*near[1:], *far_one):
        got[m] = swap(send[m], "dp", m)
    for i, m in enumerate(far_two):
        late, got[i + 1] = lax.optimization_barrier((send[m], got[i + 1]))
        got[m] = swap(late, "dp", m)

    shared = shared_rows(normed, shared_gate.T, shared_up.T, shared_down)
    def total_of(keep, give):
        return sum_rest(add(keep, swap(give, "expert", 1)))

    experts = (expert_gate[0].T, expert_up[0].T, expert_down[0])

    def join(stage):
        return jnp.concatenate([got[m] for m in stage], axis=0)

    far = join(far_one)
    far, shared = lax.optimization_barrier((far, shared))
    far_pieces = gather(far, "expert")
    mine = [got[m] for m in near]
    keep, give = expert_rows(mine + [swap(p, "expert", 1) for p in mine], *experts)
    far_pieces, keep, give = lax.optimization_barrier((far_pieces, keep, give))
    back = [None] * n_data

    def send_back(stage, rows):
        size = sizes[stage[0]]
        for i, m in enumerate(stage):
            part = rows[i * size : (i + 1) * size]
            back[m] = swap(part, "dp", m) if m else part

    send_back(near, add(keep, swap(give, "expert", 1)))
    send_back(far_one, total_of(*expert_rows(far_pieces, *experts)))
    pieces = gather(join(far_two), "expert")
    send_back(far_two, total_of(*expert_rows(pieces, *experts)))

    middle = group_rows // 2
    keep, give = [
        combine_rows(part, coef[:, rows], back, starts, BF)
        for part, rows in zip(shared, (slice(0, middle), slice(middle, None)))
    ]
    total = sum_rest(add(keep, swap(give, "expert", 1)))
    return (embed_f + total.astype(F32)).astype(BF)


def solution(mesh):
    return jax.shard_map(
        shards,
        mesh=mesh,
        in_specs=(
            P(("dp", "expert"), None),
            P(("dp", "expert"), None),
            P(("dp", "expert")),
            P(None, "expert"),
            P("expert", None),
            P(),
            P(None, "expert"),
            P(None, "expert"),
            P("expert", None),
            P("dp", None, "expert"),
            P("dp", None, "expert"),
            P("dp", "expert", None),
            P(("dp", "expert"), None),
            P(("dp", "expert"), None),
        ),
        out_specs=P(("dp", "expert"), None),
        check_vma=False,
    )
```

```python
import jax
import jax.numpy as jnp
from jax import lax
from jax.experimental import pallas as pl
from jax.experimental.pallas import tpu as pltpu
from jax.sharding import PartitionSpec as P

BF = jnp.bfloat16
F32 = jnp.float32


def dot(a, b):
    return jnp.dot(a, b, preferred_element_type=F32)


def dot_t(a, b):
    return lax.dot_general(a, b, (((1,), (1,)), ((), ())), preferred_element_type=F32)


def swap(rows, axis, mask):
    count = lax.axis_size(axis)
    return lax.ppermute(rows, axis, [(i, i ^ mask) for i in range(count)])


def gather(piece, axis):
    mask = lax.axis_size(axis) // 2
    pieces = [piece]
    while mask:
        pieces = pieces + [swap(p, axis, mask) for p in pieces]
        mask //= 2
    return pieces


def spread(piece):
    mask = lax.axis_size("expert") // 2
    pieces = [piece]
    while mask > 1:
        pieces = pieces + [swap(p, "expert", mask) for p in pieces]
        mask //= 2
    return pieces


def add(rows, other):
    return (rows.astype(F32) + other.astype(F32)).astype(BF)


def sum_rest(rows):
    mask = 2
    while mask < lax.axis_size("expert"):
        half = rows.shape[0] // 2
        rows = add(rows[:half], swap(rows[half:], "expert", mask))
        mask *= 2
    return rows


def reversed_bits(places, count):
    turned, mask, low = jnp.zeros_like(places), count // 2, 1
    while mask:
        turned += jnp.where((places & low) != 0, mask, 0)
        mask, low = mask // 2, low * 2
    return turned


def local_kernel(body, outs, args, scratch=(), macs=0):
    moved = sum(x.size * x.dtype.itemsize for x in args) + sum(
        o.size * o.dtype.itemsize for o in outs
    )
    return pl.pallas_call(
        body,
        out_shape=list(outs),
        in_specs=[pl.BlockSpec(memory_space=pltpu.VMEM)] * len(args),
        out_specs=[pl.BlockSpec(memory_space=pltpu.VMEM)] * len(outs),
        scratch_shapes=list(scratch),
        compiler_params=pltpu.CompilerParams(vmem_limit_bytes=12 * 2**20),
        cost_estimate=pl.CostEstimate(flops=2 * macs, bytes_accessed=moved, transcendentals=0),
    )(*args)


def fetch(*arrays):
    def body(*refs):
        n = len(arrays)
        sems = refs[-1]
        copies = [pltpu.make_async_copy(refs[i], refs[n + i], sems.at[i]) for i in range(n)]
        for copy in copies:
            copy.start()
        for copy in copies:
            copy.wait()

    return pl.pallas_call(
        body,
        out_shape=[jax.ShapeDtypeStruct(x.shape, x.dtype) for x in arrays],
        in_specs=[pl.BlockSpec(memory_space=pltpu.HBM)] * len(arrays),
        out_specs=[pl.BlockSpec(memory_space=pltpu.VMEM)] * len(arrays),
        scratch_shapes=[pltpu.SemaphoreType.DMA((len(arrays),))],
        compiler_params=pltpu.CompilerParams(vmem_limit_bytes=2**20),
    )(*arrays)


def fence(*values):
    return lax.optimization_barrier(values)


def put_together(refs, whole):
    at = 0
    for ref in refs:
        whole[at : at + ref.shape[0]] = ref[...]
        at += ref.shape[0]


def out(rows, columns, dtype=BF):
    return jax.ShapeDtypeStruct((rows, columns), dtype)


def steps_of(size, step):
    return size // step if size % step == 0 else 1


def gated(rows, gate, up):
    value = dot_t(rows, gate)
    return (value / (1.0 + jnp.exp(-value)) * dot_t(rows, up)).astype(BF)


def fits(pieces):
    return all(p.shape[0] % 16 == 0 for p in pieces)


def expert_rows(pieces, gate, up, down):
    count = sum(p.shape[0] for p in pieces)
    units, width = gate.shape
    if not fits(pieces) or count % 32:
        part = dot(gated(jnp.concatenate(pieces, axis=0), gate, up), down).astype(BF)
        return part[: count // 2], part[count // 2 :]

    def body(*refs):
        n = len(pieces)
        gate_ref, up_ref, down_ref, keep, give, whole = refs[n:]
        put_together(refs[:n], whole)
        if count <= 256:
            part = dot(gated(whole[...], gate_ref[...], up_ref[...]), down_ref[...])
            keep[...] = part[: count // 2].astype(BF)
            give[...] = part[count // 2 :].astype(BF)
            return
        for rows, result in ((slice(count // 2, count), give), (slice(0, count // 2), keep)):
            hidden = gated(whole[rows], gate_ref[...], up_ref[...])
            result[...] = dot(hidden, down_ref[...]).astype(BF)

    return local_kernel(
        body,
        [out(count // 2, width)] * 2,
        [*pieces, gate, up, down],
        [pltpu.VMEM((count, width), BF)],
        3 * count * width * units,
    )


def shared_rows(pieces, gate, up, down):
    count = sum(p.shape[0] for p in pieces)
    units, width = gate.shape
    if not fits(pieces):
        part = dot(gated(jnp.concatenate(pieces, axis=0), gate, up), down)
        return part[: count // 2], part[count // 2 :]

    def body(*refs):
        n = len(pieces)
        gate_ref, up_ref, down_ref, keep, give, whole = refs[n:]
        put_together(refs[:n], whole)
        part = dot(gated(whole[...], gate_ref[...], up_ref[...]), down_ref[...])
        keep[...] = part[: count // 2]
        give[...] = part[count // 2 :]

    return local_kernel(
        body,
        [out(count // 2, width, F32)] * 2,
        [*pieces, gate, up, down],
        [pltpu.VMEM((count, width), BF)],
        3 * count * width * units,
    )


def image_rows(pieces, proj_in, proj_out):
    count = sum(p.shape[0] for p in pieces)
    depth, units = proj_in.shape
    width = proj_out.shape[1]

    def body(*refs):
        n = len(pieces)
        in_ref, out_ref, keep, give, whole = refs[n:]
        put_together(refs[:n], whole)
        hidden = jax.nn.gelu(dot(whole[...], in_ref[...]), approximate=True).astype(BF)
        part = dot(hidden, out_ref[...])
        keep[...] = part[: count // 2].astype(BF)
        give[...] = part[count // 2 :].astype(BF)

    return local_kernel(
        body,
        [out(count // 2, width)] * 2,
        [*pieces, proj_in, proj_out],
        [pltpu.VMEM((count, depth), BF)],
        count * units * (depth + width),
    )


def place_rows(mine, other, place, offsets, n_data):
    count, width = mine.shape
    blocks, size = place.shape[:2]
    peer = size // n_data
    wide = width + offsets.shape[1]
    if size % 16:
        rows = jnp.concatenate([add(mine, other), offsets], axis=1).reshape(blocks, size, wide)
        moved = jnp.einsum("bsr,brw->bsw", place, rows, preferred_element_type=F32).astype(BF)
        return moved.reshape(blocks, n_data, peer, wide).swapaxes(0, 1).reshape(n_data, -1, wide)

    def body(mine_ref, other_ref, place_ref, offsets_ref, result):
        moved, beside = [], []
        for b in range(blocks):
            span = slice(b * size, (b + 1) * size)
            moved.append(dot(place_ref[b], add(mine_ref[span], other_ref[span])))
            beside.append(dot(place_ref[b], offsets_ref[span]))
        for d in range(n_data):
            part = slice(d * peer, (d + 1) * peer)
            result[d, :, :width] = jnp.concatenate([m[part] for m in moved], axis=0).astype(BF)
            result[d, :, width:] = jnp.concatenate([m[part] for m in beside], axis=0).astype(BF)

    return local_kernel(
        body,
        [jax.ShapeDtypeStruct((n_data, blocks * peer, wide), BF)],
        [mine, other, place, offsets],
        (),
        count * size * wide,
    )[0]


def embed_rows(pieces, texts, gain, peer):
    n_data, stack, wide = pieces[0].shape
    count, width = texts[0].shape
    blocks = len(texts)
    total_rows, total = n_data * stack, blocks * count

    def in_order(piece, p):
        order = [p ^ b for b in range(blocks)]
        return piece if p == 0 else jnp.concatenate([piece[o * peer : (o + 1) * peer] for o in order], axis=0)

    def math(parts, text, gain_row):
        rows = parts[0][:, :width]
        for part in parts[1:]:
            rows = rows + part[:, :width]
        line = lax.broadcasted_iota(jnp.int32, (total_rows, 1), 0)
        target = parts[0][:, width : width + 1] + (line // peer % blocks * count).astype(F32)
        spots = lax.broadcasted_iota(jnp.int32, (1, total), 1).astype(F32) == target
        spots = spots.astype(F32)
        turned = (((0,), (0,)), ((), ()))
        placed = lax.dot_general(spots.astype(BF), rows.astype(BF), turned, preferred_element_type=F32)
        named = lax.dot_general(spots, jnp.ones_like(target), turned, preferred_element_type=F32)
        embed = jnp.where(named > 0.5, placed, text.astype(F32))
        meansq = jnp.mean(embed * embed, axis=-1, keepdims=True) + 1e-06
        return embed[:count], (embed * lax.rsqrt(meansq) * gain_row).astype(BF)

    gain = gain.reshape(1, width)
    if stack % 8:
        parts = [
            jnp.concatenate([in_order(piece[d], p) for d in range(n_data)], axis=0).astype(F32)
            for p, piece in enumerate(pieces)
        ]
        return math(parts, jnp.concatenate(texts, axis=0), gain)

    def body(*refs):
        gain_ref, embed_ref, normed_ref = refs[2 * blocks :]
        parts = [
            jnp.concatenate([in_order(ref[d].astype(F32), p) for d in range(n_data)], axis=0)
            for p, ref in enumerate(refs[:blocks])
        ]
        text = jnp.concatenate([ref[...].astype(F32) for ref in refs[blocks : 2 * blocks]], axis=0)
        embed_ref[...], normed_ref[...] = math(parts, text, gain_ref[...])

    return local_kernel(
        body,
        [out(count, width, F32), out(total, width)],
        [*pieces, *texts, gain],
        (),
        total * total_rows * width,
    )


def pick_rows(picks, pieces, starts, sizes):
    count, width = sum(p.shape[0] for p in pieces), pieces[0].shape[1]
    if not fits(pieces) or any(n % 8 for n in (*starts, *sizes)):
        rows = dot(picks, jnp.concatenate(pieces, axis=0)).astype(BF)
        return [rows[at : at + size] for at, size in zip(starts, sizes)]

    def body(*refs):
        n = len(pieces)
        whole = refs[-1]
        put_together(refs[1 : n + 1], whole)
        rows = dot(refs[0][...], whole[...])
        for ref, at, size in zip(refs[n + 1 : -1], starts, sizes):
            ref[...] = rows[at : at + size].astype(BF)

    return local_kernel(
        body,
        [out(size, width) for size in sizes],
        [picks, *pieces],
        [pltpu.VMEM((count, width), BF)],
        picks.shape[0] * count * width,
    )


def combine_rows(total, coef, backs, starts, dtype):
    count, width = total.shape
    slots = coef.shape[2]
    ends = list(starts[1:]) + [slots]
    if any(n % 16 for n in (slots, *starts)):
        whole = jnp.concatenate(
            [jnp.pad(b, ((0, e - s - b.shape[0]), (0, 0))) for b, s, e in zip(backs, starts, ends)],
            axis=0,
        )
        return (total + dot(coef[0], whole) + dot(coef[1], whole)).astype(dtype)

    def body(*refs):
        total_ref, coef_ref, result, whole = refs[0], refs[1], refs[-2], refs[-1]
        for ref, at, end in zip(refs[2:-2], starts, ends):
            size = ref.shape[0]
            if size != end - at:
                whole[end - 16 : end] = jnp.zeros((16, width), BF)
            whole[at : at + size] = ref[...]
        rows = whole[...]
        value = total_ref[...] + dot(coef_ref[0], rows)
        result[...] = (value + dot(coef_ref[1], rows)).astype(dtype)

    return local_kernel(
        body,
        [out(count, width, dtype)],
        [total, coef, *backs],
        [pltpu.VMEM((slots, width), BF)],
        2 * count * width * slots,
    )[0]


def one_hot(places, count):
    return places[None, :] == jnp.arange(count, dtype=jnp.int32)[:, None]


def shards(
    text_embed,
    image_feats,
    tile_pos,
    proj_in,
    proj_out,
    norm_gain,
    shared_gate,
    shared_up,
    shared_down,
    expert_gate,
    expert_up,
    expert_down,
    route_ids,
    route_wts,
):
    tok_dev, width = text_embed.shape
    img_dev = image_feats.shape[0]
    n_data = lax.axis_size("dp")
    n_group = lax.axis_size("expert")
    peer = img_dev // n_data
    my_place = lax.axis_index("expert")
    top = route_ids.shape[1]
    group_rows = tok_dev * n_group
    capacity = 3 * group_rows * top // (2 * n_data)
    share = capacity // n_group

    weights_in, weights_out, own_feats = fetch(proj_in, proj_out, image_feats)
    routes = spread(jnp.concatenate([route_ids, route_wts], axis=1))
    spots, feats = spread(tile_pos), spread(image_feats)
    partner = [swap(image_feats, "expert", 1)]
    feats, partner, spots, routes, own_feats = fence(feats, partner, spots, routes, own_feats)
    feats = feats + partner + [swap(p, "expert", 1) for p in feats[1:]]
    keep, give = image_rows([own_feats, *feats[1:]], weights_in, weights_out)

    spots, keep, give = fence(spots, keep, give)
    spots = jnp.stack(spots)
    owner = spots // tok_dev // n_group
    earlier = jnp.arange(img_dev)[None, :] < jnp.arange(img_dev)[:, None]
    rank_img = jnp.sum(((owner[:, :, None] == owner[:, None, :]) & earlier).astype(jnp.int32), axis=2)
    seat = owner * peer + rank_img
    place = (seat[:, None, :] == jnp.arange(img_dev, dtype=jnp.int32)[None, :, None]).astype(BF)
    offsets = jnp.broadcast_to((spots % tok_dev).astype(BF).reshape(-1, 1), (spots.size, 128))
    leaving = place_rows(keep, swap(give, "expert", 1), place, offsets, n_data)
    texts, routes, leaving = fence(text_embed, routes, leaving)
    texts = spread(texts)
    routes = routes + [swap(p, "expert", 1) for p in routes]
    arrived = lax.all_to_all(leaving, "dp", split_axis=0, concat_axis=0, tiled=True)
    texts, routes, arrived = fence(texts, routes, arrived)
    embed_f, normed = embed_rows(spread(arrived), texts, norm_gain, peer)
    normed = [normed, swap(normed, "expert", 1)]

    routes = jnp.concatenate(routes, axis=0)
    ids, weights = routes[:, :top], routes[:, top:].astype(F32)
    weights = weights / jnp.sum(weights, axis=1, keepdims=True)
    rows_at = jnp.arange(group_rows, dtype=jnp.int32)
    token = (my_place ^ reversed_bits(rows_at // tok_dev, n_group)) * tok_dev + rows_at % tok_dev
    named = ids[:, :, None] == jnp.arange(n_data, dtype=jnp.int32)[None, None, :]
    before = token[None, :] < token[:, None]
    counts = dot(before.astype(BF), jnp.any(named, axis=1).astype(BF))
    rank = jnp.sum(jnp.where(named, counts[:, None, :], 0.0), axis=2).astype(jnp.int32)
    distance = ids ^ lax.axis_index("dp")

    half = n_data // 2
    wide = 2 * capacity // 4
    core = my_place % 2
    near_slot = jnp.where((distance < half) & (rank // wide == core), distance * wide + rank % wide, -1)
    apart = -(-share // 16) * 16
    far_slot = jnp.where(
        (distance >= half) & (rank // share == my_place),
        (distance - half) * apart + rank % share + half * wide,
        -1,
    )
    slot = jnp.maximum(near_slot, far_slot)
    sizes = [wide] * half + [share] * (n_data - half)
    starts = [m * wide if m < half else half * wide + (m - half) * apart for m in range(n_data)]
    slots = half * wide + (n_data - half) * apart
    hits = [one_hot(slot[:, k], slots) for k in range(top)]
    picks = sum(hit.astype(BF) for hit in hits)
    coef = sum(jnp.where(hit, weights[:, k][None, :], 0.0) for k, hit in enumerate(hits)).T
    coef_hi = coef.astype(BF)
    coef = jnp.stack([coef_hi, (coef - coef_hi.astype(F32)).astype(BF)])

    send = pick_rows(picks, normed, starts, sizes)
    got = [None] * n_data
    got[0] = send[0]
    quarter = n_data // 4
    near, far_one, far_two = range(half), range(half, half + quarter), range(half + quarter, n_data)

    def join(stage):
        return jnp.concatenate([got[m] for m in stage], axis=0)

    def both(pieces):
        return pieces + [swap(p, "expert", 1) for p in pieces]

    def send_back(m, rows, i):
        part = rows[i * sizes[m] : (i + 1) * sizes[m]]
        return swap(part, "dp", m) if m else part

    for m in (*near[1:], *far_one):
        got[m] = swap(send[m], "dp", m)
    shared = shared_rows(normed, shared_gate.T, shared_up.T, shared_down)
    one, shared, send = fence(join(far_one), shared, send)

    for m in far_two:
        got[m] = swap(send[m], "dp", m)
    one, got = fence(spread(one), got)

    experts = (expert_gate[0].T, expert_up[0].T, expert_down[0])
    one_keep, one_give = expert_rows(both(one), *experts)
    two, one_keep, one_give = fence(spread(join(far_two)), one_keep, one_give)
    two_keep, two_give = expert_rows(both(two), *experts)
    mine = join(near)
    mine = [mine, swap(mine, "expert", 1)]
    mine, two_keep = fence(mine, two_keep)
    keep, give = expert_rows(mine, *experts)
    one = sum_rest(add(one_keep, swap(one_give, "expert", 1)))
    one, keep, give = fence(one, keep, give)
    two = sum_rest(add(two_keep, swap(two_give, "expert", 1)))
    rows = add(keep, swap(give, "expert", 1))
    back = [send_back(m, rows, m) for m in near]
    back += [send_back(m, one, i) for i, m in enumerate(far_one)]
    back += [send_back(m, two, i) for i, m in enumerate(far_two)]

    middle = group_rows // 2
    keep, give = [
        combine_rows(part, coef[:, rows], back, starts, BF)
        for part, rows in zip(shared, (slice(0, middle), slice(middle, None)))
    ]
    total = sum_rest(add(keep, swap(give, "expert", 1)))
    return (embed_f + total.astype(F32)).astype(BF)


def solution(mesh):
    return jax.shard_map(
        shards,
        mesh=mesh,
        in_specs=(
            P(("dp", "expert"), None),
            P(("dp", "expert"), None),
            P(("dp", "expert")),
            P(None, "expert"),
            P("expert", None),
            P(),
            P(None, "expert"),
            P(None, "expert"),
            P("expert", None),
            P("dp", None, "expert"),
            P("dp", None, "expert"),
            P("dp", "expert", None),
            P(("dp", "expert"), None),
            P(("dp", "expert"), None),
        ),
        out_specs=P(("dp", "expert"), None),
        check_vma=False,
    )
```

```python
import jax
import jax.numpy as jnp
from jax import lax
from jax.experimental import pallas as pl
from jax.experimental.pallas import tpu as pltpu
from jax.sharding import PartitionSpec as P

BF = jnp.bfloat16
F32 = jnp.float32


def dot(a, b):
    return jnp.dot(a, b, preferred_element_type=F32)


def dot_t(a, b):
    return lax.dot_general(a, b, (((1,), (1,)), ((), ())), preferred_element_type=F32)


def swap(rows, axis, mask):
    count = lax.axis_size(axis)
    return lax.ppermute(rows, axis, [(i, i ^ mask) for i in range(count)])


def gather(piece, axis):
    mask = lax.axis_size(axis) // 2
    pieces = [piece]
    while mask:
        pieces = pieces + [swap(p, axis, mask) for p in pieces]
        mask //= 2
    return pieces


def spread(piece):
    mask = lax.axis_size("expert") // 2
    pieces = [piece]
    while mask > 1:
        pieces = pieces + [swap(p, "expert", mask) for p in pieces]
        mask //= 2
    return pieces


def add(rows, other):
    return (rows.astype(F32) + other.astype(F32)).astype(BF)


def sum_rest(rows):
    mask = 2
    while mask < lax.axis_size("expert"):
        half = rows.shape[0] // 2
        rows = add(rows[:half], swap(rows[half:], "expert", mask))
        mask *= 2
    return rows


def reversed_bits(places, count):
    turned, mask, low = jnp.zeros_like(places), count // 2, 1
    while mask:
        turned += jnp.where((places & low) != 0, mask, 0)
        mask, low = mask // 2, low * 2
    return turned


def local_kernel(body, outs, args, scratch=(), macs=0):
    moved = sum(x.size * x.dtype.itemsize for x in args) + sum(
        o.size * o.dtype.itemsize for o in outs
    )
    return pl.pallas_call(
        body,
        out_shape=list(outs),
        in_specs=[pl.BlockSpec(memory_space=pltpu.VMEM)] * len(args),
        out_specs=[pl.BlockSpec(memory_space=pltpu.VMEM)] * len(outs),
        scratch_shapes=list(scratch),
        compiler_params=pltpu.CompilerParams(vmem_limit_bytes=12 * 2**20),
        cost_estimate=pl.CostEstimate(flops=2 * macs, bytes_accessed=moved, transcendentals=0),
    )(*args)


def fetch(*arrays):
    def body(*refs):
        n = len(arrays)
        sems = refs[-1]
        copies = [pltpu.make_async_copy(refs[i], refs[n + i], sems.at[i]) for i in range(n)]
        for copy in copies:
            copy.start()
        for copy in copies:
            copy.wait()

    return pl.pallas_call(
        body,
        out_shape=[jax.ShapeDtypeStruct(x.shape, x.dtype) for x in arrays],
        in_specs=[pl.BlockSpec(memory_space=pltpu.HBM)] * len(arrays),
        out_specs=[pl.BlockSpec(memory_space=pltpu.VMEM)] * len(arrays),
        scratch_shapes=[pltpu.SemaphoreType.DMA((len(arrays),))],
        compiler_params=pltpu.CompilerParams(vmem_limit_bytes=2**20),
    )(*arrays)


def fence(*values):
    return lax.optimization_barrier(values)


def put_together(refs, whole):
    at = 0
    for ref in refs:
        whole[at : at + ref.shape[0]] = ref[...]
        at += ref.shape[0]


def out(rows, columns, dtype=BF):
    return jax.ShapeDtypeStruct((rows, columns), dtype)


def steps_of(size, step):
    return size // step if size % step == 0 else 1


def gated(rows, gate, up):
    value = dot_t(rows, gate)
    return (value / (1.0 + jnp.exp(-value)) * dot_t(rows, up)).astype(BF)


def fits(pieces):
    return all(p.shape[0] % 16 == 0 for p in pieces)


def expert_rows(pieces, gate, up, down):
    count = sum(p.shape[0] for p in pieces)
    units, width = gate.shape
    if not fits(pieces) or count % 32:
        part = dot(gated(jnp.concatenate(pieces, axis=0), gate, up), down).astype(BF)
        return part[: count // 2], part[count // 2 :]

    def body(*refs):
        n = len(pieces)
        gate_ref, up_ref, down_ref, keep, give, whole = refs[n:]
        put_together(refs[:n], whole)
        if count <= 256:
            part = dot(gated(whole[...], gate_ref[...], up_ref[...]), down_ref[...])
            keep[...] = part[: count // 2].astype(BF)
            give[...] = part[count // 2 :].astype(BF)
            return
        for rows, result in ((slice(count // 2, count), give), (slice(0, count // 2), keep)):
            hidden = gated(whole[rows], gate_ref[...], up_ref[...])
            result[...] = dot(hidden, down_ref[...]).astype(BF)

    return local_kernel(
        body,
        [out(count // 2, width)] * 2,
        [*pieces, gate, up, down],
        [pltpu.VMEM((count, width), BF)],
        3 * count * width * units,
    )


def shared_rows(pieces, gate, up, down):
    count = sum(p.shape[0] for p in pieces)
    units, width = gate.shape
    if not fits(pieces):
        part = dot(gated(jnp.concatenate(pieces, axis=0), gate, up), down)
        return part[: count // 2], part[count // 2 :]

    def body(*refs):
        n = len(pieces)
        gate_ref, up_ref, down_ref, keep, give, whole = refs[n:]
        put_together(refs[:n], whole)
        part = dot(gated(whole[...], gate_ref[...], up_ref[...]), down_ref[...])
        keep[...] = part[: count // 2]
        give[...] = part[count // 2 :]

    return local_kernel(
        body,
        [out(count // 2, width, F32)] * 2,
        [*pieces, gate, up, down],
        [pltpu.VMEM((count, width), BF)],
        3 * count * width * units,
    )


def image_rows(pieces, proj_in, proj_out):
    count = sum(p.shape[0] for p in pieces)
    depth, units = proj_in.shape
    width = proj_out.shape[1]

    def body(*refs):
        n = len(pieces)
        in_ref, out_ref, keep, give, whole = refs[n:]
        put_together(refs[:n], whole)
        hidden = jax.nn.gelu(dot(whole[...], in_ref[...]), approximate=True).astype(BF)
        part = dot(hidden, out_ref[...])
        keep[...] = part[: count // 2].astype(BF)
        give[...] = part[count // 2 :].astype(BF)

    return local_kernel(
        body,
        [out(count // 2, width)] * 2,
        [*pieces, proj_in, proj_out],
        [pltpu.VMEM((count, depth), BF)],
        count * units * (depth + width),
    )


def place_rows(mine, other, place, offsets, n_data):
    count, width = mine.shape
    blocks, size = place.shape[:2]
    peer = size // n_data
    wide = width + offsets.shape[1]
    if size % 16:
        rows = jnp.concatenate([add(mine, other), offsets], axis=1).reshape(blocks, size, wide)
        moved = jnp.einsum("bsr,brw->bsw", place, rows, preferred_element_type=F32).astype(BF)
        return moved.reshape(blocks, n_data, peer, wide).swapaxes(0, 1).reshape(n_data, -1, wide)

    def body(mine_ref, other_ref, place_ref, offsets_ref, result):
        moved, beside = [], []
        for b in range(blocks):
            span = slice(b * size, (b + 1) * size)
            moved.append(dot(place_ref[b], add(mine_ref[span], other_ref[span])))
            beside.append(dot(place_ref[b], offsets_ref[span]))
        for d in range(n_data):
            part = slice(d * peer, (d + 1) * peer)
            result[d, :, :width] = jnp.concatenate([m[part] for m in moved], axis=0).astype(BF)
            result[d, :, width:] = jnp.concatenate([m[part] for m in beside], axis=0).astype(BF)

    return local_kernel(
        body,
        [jax.ShapeDtypeStruct((n_data, blocks * peer, wide), BF)],
        [mine, other, place, offsets],
        (),
        count * size * wide,
    )[0]


def embed_rows(pieces, texts, gain, peer):
    n_data, stack, wide = pieces[0].shape
    count, width = texts[0].shape
    blocks = len(texts)
    total_rows, total = n_data * stack, blocks * count

    def in_order(piece, p):
        order = [p ^ b for b in range(blocks)]
        return piece if p == 0 else jnp.concatenate([piece[o * peer : (o + 1) * peer] for o in order], axis=0)

    def math(parts, text, gain_row):
        rows = parts[0][:, :width]
        for part in parts[1:]:
            rows = rows + part[:, :width]
        line = lax.broadcasted_iota(jnp.int32, (total_rows, 1), 0)
        target = parts[0][:, width : width + 1] + (line // peer % blocks * count).astype(F32)
        spots = lax.broadcasted_iota(jnp.int32, (1, total), 1).astype(F32) == target
        spots = spots.astype(F32)
        turned = (((0,), (0,)), ((), ()))
        placed = lax.dot_general(spots.astype(BF), rows.astype(BF), turned, preferred_element_type=F32)
        named = lax.dot_general(spots, jnp.ones_like(target), turned, preferred_element_type=F32)
        embed = jnp.where(named > 0.5, placed, text.astype(F32))
        meansq = jnp.mean(embed * embed, axis=-1, keepdims=True) + 1e-06
        return embed[:count], (embed * lax.rsqrt(meansq) * gain_row).astype(BF)

    gain = gain.reshape(1, width)
    if stack % 8:
        parts = [
            jnp.concatenate([in_order(piece[d], p) for d in range(n_data)], axis=0).astype(F32)
            for p, piece in enumerate(pieces)
        ]
        return math(parts, jnp.concatenate(texts, axis=0), gain)

    def body(*refs):
        gain_ref, embed_ref, normed_ref = refs[2 * blocks :]
        parts = [
            jnp.concatenate([in_order(ref[d].astype(F32), p) for d in range(n_data)], axis=0)
            for p, ref in enumerate(refs[:blocks])
        ]
        text = jnp.concatenate([ref[...].astype(F32) for ref in refs[blocks : 2 * blocks]], axis=0)
        embed_ref[...], normed_ref[...] = math(parts, text, gain_ref[...])

    return local_kernel(
        body,
        [out(count, width, F32), out(total, width)],
        [*pieces, *texts, gain],
        (),
        total * total_rows * width,
    )


def pick_rows(picks, pieces, starts, sizes):
    count, width = sum(p.shape[0] for p in pieces), pieces[0].shape[1]
    if not fits(pieces) or any(n % 8 for n in (*starts, *sizes)):
        rows = dot(picks, jnp.concatenate(pieces, axis=0)).astype(BF)
        return [rows[at : at + size] for at, size in zip(starts, sizes)]

    def body(*refs):
        n = len(pieces)
        whole = refs[-1]
        put_together(refs[1 : n + 1], whole)
        rows = dot(refs[0][...], whole[...])
        for ref, at, size in zip(refs[n + 1 : -1], starts, sizes):
            ref[...] = rows[at : at + size].astype(BF)

    return local_kernel(
        body,
        [out(size, width) for size in sizes],
        [picks, *pieces],
        [pltpu.VMEM((count, width), BF)],
        picks.shape[0] * count * width,
    )


def combine_rows(total, coef, backs, starts, dtype):
    count, width = total.shape
    slots = coef.shape[2]
    ends = list(starts[1:]) + [slots]
    if any(n % 16 for n in (slots, *starts)):
        whole = jnp.concatenate(
            [jnp.pad(b, ((0, e - s - b.shape[0]), (0, 0))) for b, s, e in zip(backs, starts, ends)],
            axis=0,
        )
        return (total + dot(coef[0], whole) + dot(coef[1], whole)).astype(dtype)

    def body(*refs):
        total_ref, coef_ref, result, whole = refs[0], refs[1], refs[-2], refs[-1]
        for ref, at, end in zip(refs[2:-2], starts, ends):
            size = ref.shape[0]
            if size != end - at:
                whole[end - 16 : end] = jnp.zeros((16, width), BF)
            whole[at : at + size] = ref[...]
        rows = whole[...]
        value = total_ref[...] + dot(coef_ref[0], rows)
        result[...] = (value + dot(coef_ref[1], rows)).astype(dtype)

    return local_kernel(
        body,
        [out(count, width, dtype)],
        [total, coef, *backs],
        [pltpu.VMEM((slots, width), BF)],
        2 * count * width * slots,
    )[0]


def one_hot(places, count):
    return places[None, :] == jnp.arange(count, dtype=jnp.int32)[:, None]


def shards(
    text_embed,
    image_feats,
    tile_pos,
    proj_in,
    proj_out,
    norm_gain,
    shared_gate,
    shared_up,
    shared_down,
    expert_gate,
    expert_up,
    expert_down,
    route_ids,
    route_wts,
):
    tok_dev, width = text_embed.shape
    img_dev = image_feats.shape[0]
    n_data = lax.axis_size("dp")
    n_group = lax.axis_size("expert")
    peer = img_dev // n_data
    my_place = lax.axis_index("expert")
    top = route_ids.shape[1]
    group_rows = tok_dev * n_group
    capacity = 3 * group_rows * top // (2 * n_data)
    share = capacity // n_group

    weights_in, weights_out, own_feats = fetch(proj_in, proj_out, image_feats)
    routes = spread(jnp.concatenate([route_ids, route_wts], axis=1))
    spots, feats = spread(tile_pos), spread(image_feats)
    partner = [swap(image_feats, "expert", 1)]
    feats, partner, spots, routes, own_feats = fence(feats, partner, spots, routes, own_feats)
    feats = feats + partner + [swap(p, "expert", 1) for p in feats[1:]]
    keep, give = image_rows([own_feats, *feats[1:]], weights_in, weights_out)

    spots, keep, give = fence(spots, keep, give)
    spots = jnp.stack(spots)
    owner = spots // tok_dev // n_group
    earlier = jnp.arange(img_dev)[None, :] < jnp.arange(img_dev)[:, None]
    rank_img = jnp.sum(((owner[:, :, None] == owner[:, None, :]) & earlier).astype(jnp.int32), axis=2)
    seat = owner * peer + rank_img
    place = (seat[:, None, :] == jnp.arange(img_dev, dtype=jnp.int32)[None, :, None]).astype(BF)
    offsets = jnp.broadcast_to((spots % tok_dev).astype(BF).reshape(-1, 1), (spots.size, 128))
    leaving = place_rows(keep, swap(give, "expert", 1), place, offsets, n_data)
    texts, routes, leaving = fence(text_embed, routes, leaving)
    texts = spread(texts)
    routes = routes + [swap(p, "expert", 1) for p in routes]
    arrived = lax.all_to_all(leaving, "dp", split_axis=0, concat_axis=0, tiled=True)
    texts, routes, arrived = fence(texts, routes, arrived)
    embed_f, normed = embed_rows(spread(arrived), texts, norm_gain, peer)
    normed = [normed, swap(normed, "expert", 1)]

    routes = jnp.concatenate(routes, axis=0)
    ids, weights = routes[:, :top], routes[:, top:].astype(F32)
    weights = weights / jnp.sum(weights, axis=1, keepdims=True)
    rows_at = jnp.arange(group_rows, dtype=jnp.int32)
    token = (my_place ^ reversed_bits(rows_at // tok_dev, n_group)) * tok_dev + rows_at % tok_dev
    named = ids[:, :, None] == jnp.arange(n_data, dtype=jnp.int32)[None, None, :]
    before = token[None, :] < token[:, None]
    counts = dot(before.astype(BF), jnp.any(named, axis=1).astype(BF))
    rank = jnp.sum(jnp.where(named, counts[:, None, :], 0.0), axis=2).astype(jnp.int32)
    distance = ids ^ lax.axis_index("dp")

    half = n_data // 2
    wide = 2 * capacity // 4
    core = my_place % 2
    near_slot = jnp.where((distance < half) & (rank // wide == core), distance * wide + rank % wide, -1)
    apart = -(-share // 16) * 16
    far_slot = jnp.where(
        (distance >= half) & (rank // share == my_place),
        (distance - half) * apart + rank % share + half * wide,
        -1,
    )
    slot = jnp.maximum(near_slot, far_slot)
    sizes = [wide] * half + [share] * (n_data - half)
    starts = [m * wide if m < half else half * wide + (m - half) * apart for m in range(n_data)]
    slots = half * wide + (n_data - half) * apart
    hits = [one_hot(slot[:, k], slots) for k in range(top)]
    picks = sum(hit.astype(BF) for hit in hits)
    coef = sum(jnp.where(hit, weights[:, k][None, :], 0.0) for k, hit in enumerate(hits)).T
    coef_hi = coef.astype(BF)
    coef = jnp.stack([coef_hi, (coef - coef_hi.astype(F32)).astype(BF)])

    send = pick_rows(picks, normed, starts, sizes)
    got = [None] * n_data
    got[0] = send[0]
    quarter = n_data // 4
    near, far_one, far_two = range(half), range(half, half + quarter), range(half + quarter, n_data)

    def join(stage):
        return jnp.concatenate([got[m] for m in stage], axis=0)

    def both(pieces):
        return pieces + [swap(p, "expert", 1) for p in pieces]

    def send_back(m, rows, i):
        part = rows[i * sizes[m] : (i + 1) * sizes[m]]
        return swap(part, "dp", m) if m else part

    for m in (*near[1:], *far_one):
        got[m] = swap(send[m], "dp", m)
    one, send = fence(join(far_one), send)

    for m in far_two:
        got[m] = swap(send[m], "dp", m)
    one, got = fence(spread(one), got)

    experts = (expert_gate[0].T, expert_up[0].T, expert_down[0])
    one_keep, one_give = expert_rows(both(one), *experts)
    two, one_keep, one_give = fence(spread(join(far_two)), one_keep, one_give)
    two_keep, two_give = expert_rows(both(two), *experts)
    mine = join(near)
    mine = [mine, swap(mine, "expert", 1)]
    mine, two_keep = fence(mine, two_keep)
    keep, give = expert_rows(mine, *experts)
    one = sum_rest(add(one_keep, swap(one_give, "expert", 1)))
    one, keep, give, normed = fence(one, keep, give, normed)
    two = sum_rest(add(two_keep, swap(two_give, "expert", 1)))
    rows = add(keep, swap(give, "expert", 1))
    back = [send_back(m, rows, m) for m in near]
    back += [send_back(m, one, i) for i, m in enumerate(far_one)]
    back += [send_back(m, two, i) for i, m in enumerate(far_two)]
    shared = shared_rows(normed, shared_gate.T, shared_up.T, shared_down)

    middle = group_rows // 2
    keep, give = [
        combine_rows(part, coef[:, rows], back, starts, BF)
        for part, rows in zip(shared, (slice(0, middle), slice(middle, None)))
    ]
    total = sum_rest(add(keep, swap(give, "expert", 1)))
    return (embed_f + total.astype(F32)).astype(BF)


def solution(mesh):
    return jax.shard_map(
        shards,
        mesh=mesh,
        in_specs=(
            P(("dp", "expert"), None),
            P(("dp", "expert"), None),
            P(("dp", "expert")),
            P(None, "expert"),
            P("expert", None),
            P(),
            P(None, "expert"),
            P(None, "expert"),
            P("expert", None),
            P("dp", None, "expert"),
            P("dp", None, "expert"),
            P("dp", "expert", None),
            P(("dp", "expert"), None),
            P(("dp", "expert"), None),
        ),
        out_specs=P(("dp", "expert"), None),
        check_vma=False,
    )
```

```python
import jax
import jax.numpy as jnp
from jax import lax
from jax.experimental import pallas as pl
from jax.experimental.pallas import tpu as pltpu
from jax.sharding import PartitionSpec as P

BF = jnp.bfloat16
F32 = jnp.float32


def dot(a, b):
    return jnp.dot(a, b, preferred_element_type=F32)


def dot_t(a, b):
    return lax.dot_general(a, b, (((1,), (1,)), ((), ())), preferred_element_type=F32)


def swap(rows, axis, mask):
    count = lax.axis_size(axis)
    return lax.ppermute(rows, axis, [(i, i ^ mask) for i in range(count)])


def gather(piece, axis):
    mask = lax.axis_size(axis) // 2
    pieces = [piece]
    while mask:
        pieces = pieces + [swap(p, axis, mask) for p in pieces]
        mask //= 2
    return pieces


def spread(piece):
    mask = lax.axis_size("expert") // 2
    pieces = [piece]
    while mask > 1:
        pieces = pieces + [swap(p, "expert", mask) for p in pieces]
        mask //= 2
    return pieces


def add(rows, other):
    return (rows.astype(F32) + other.astype(F32)).astype(BF)


def sum_rest(rows):
    mask = 2
    while mask < lax.axis_size("expert"):
        half = rows.shape[0] // 2
        rows = add(rows[:half], swap(rows[half:], "expert", mask))
        mask *= 2
    return rows


def reversed_bits(places, count):
    turned, mask, low = jnp.zeros_like(places), count // 2, 1
    while mask:
        turned += jnp.where((places & low) != 0, mask, 0)
        mask, low = mask // 2, low * 2
    return turned


def local_kernel(body, outs, args, scratch=(), macs=0):
    moved = sum(x.size * x.dtype.itemsize for x in args) + sum(
        o.size * o.dtype.itemsize for o in outs
    )
    return pl.pallas_call(
        body,
        out_shape=list(outs),
        in_specs=[pl.BlockSpec(memory_space=pltpu.VMEM)] * len(args),
        out_specs=[pl.BlockSpec(memory_space=pltpu.VMEM)] * len(outs),
        scratch_shapes=list(scratch),
        compiler_params=pltpu.CompilerParams(vmem_limit_bytes=12 * 2**20),
        cost_estimate=pl.CostEstimate(flops=2 * macs, bytes_accessed=moved, transcendentals=0),
    )(*args)


def fetch(*arrays):
    def body(*refs):
        n = len(arrays)
        sems = refs[-1]
        copies = [pltpu.make_async_copy(refs[i], refs[n + i], sems.at[i]) for i in range(n)]
        for copy in copies:
            copy.start()
        for copy in copies:
            copy.wait()

    return pl.pallas_call(
        body,
        out_shape=[jax.ShapeDtypeStruct(x.shape, x.dtype) for x in arrays],
        in_specs=[pl.BlockSpec(memory_space=pltpu.HBM)] * len(arrays),
        out_specs=[pl.BlockSpec(memory_space=pltpu.VMEM)] * len(arrays),
        scratch_shapes=[pltpu.SemaphoreType.DMA((len(arrays),))],
        compiler_params=pltpu.CompilerParams(vmem_limit_bytes=2**20),
    )(*arrays)


def fence(*values):
    return lax.optimization_barrier(values)


def put_together(refs, whole):
    at = 0
    for ref in refs:
        whole[at : at + ref.shape[0]] = ref[...]
        at += ref.shape[0]


def out(rows, columns, dtype=BF):
    return jax.ShapeDtypeStruct((rows, columns), dtype)


def steps_of(size, step):
    return size // step if size % step == 0 else 1


def gated(rows, gate, up):
    value = dot_t(rows, gate)
    return (value / (1.0 + jnp.exp(-value)) * dot_t(rows, up)).astype(BF)


def fits(pieces):
    return all(p.shape[0] % 16 == 0 for p in pieces)


def expert_rows(pieces, gate, up, down, order=None):
    count = sum(p.shape[0] for p in pieces)
    units, width = gate.shape

    def in_order(rows):
        if order is None:
            return rows
        return jnp.concatenate([rows[at : at + size] for at, size in order], axis=0)

    if not fits(pieces) or count % 32:
        part = dot(gated(jnp.concatenate(pieces, axis=0), gate, up), down).astype(BF)
        return in_order(part[: count // 2]), in_order(part[count // 2 :])

    def body(*refs):
        n = len(pieces)
        gate_ref, up_ref, down_ref, keep, give, whole = refs[n:]
        put_together(refs[:n], whole)
        if count <= 256:
            part = dot(gated(whole[...], gate_ref[...], up_ref[...]), down_ref[...])
            keep[...] = in_order(part[: count // 2]).astype(BF)
            give[...] = in_order(part[count // 2 :]).astype(BF)
            return
        for rows, result in ((slice(count // 2, count), give), (slice(0, count // 2), keep)):
            hidden = gated(whole[rows], gate_ref[...], up_ref[...])
            result[...] = in_order(dot(hidden, down_ref[...])).astype(BF)

    return local_kernel(
        body,
        [out(count // 2, width)] * 2,
        [*pieces, gate, up, down],
        [pltpu.VMEM((count, width), BF)],
        3 * count * width * units,
    )


def shared_rows(pieces, gate, up, down):
    count = sum(p.shape[0] for p in pieces)
    units, width = gate.shape
    if not fits(pieces):
        part = dot(gated(jnp.concatenate(pieces, axis=0), gate, up), down)
        return part[: count // 2], part[count // 2 :]

    def body(*refs):
        n = len(pieces)
        gate_ref, up_ref, down_ref, keep, give, whole = refs[n:]
        put_together(refs[:n], whole)
        part = dot(gated(whole[...], gate_ref[...], up_ref[...]), down_ref[...])
        keep[...] = part[: count // 2]
        give[...] = part[count // 2 :]

    return local_kernel(
        body,
        [out(count // 2, width, F32)] * 2,
        [*pieces, gate, up, down],
        [pltpu.VMEM((count, width), BF)],
        3 * count * width * units,
    )


def image_rows(pieces, proj_in, proj_out):
    count = sum(p.shape[0] for p in pieces)
    depth, units = proj_in.shape
    width = proj_out.shape[1]

    def body(*refs):
        n = len(pieces)
        in_ref, out_ref, keep, give, whole = refs[n:]
        put_together(refs[:n], whole)
        hidden = jax.nn.gelu(dot(whole[...], in_ref[...]), approximate=True).astype(BF)
        part = dot(hidden, out_ref[...])
        keep[...] = part[: count // 2].astype(BF)
        give[...] = part[count // 2 :].astype(BF)

    return local_kernel(
        body,
        [out(count // 2, width)] * 2,
        [*pieces, proj_in, proj_out],
        [pltpu.VMEM((count, depth), BF)],
        count * units * (depth + width),
    )


def place_rows(mine, other, place, offsets, n_data):
    count, width = mine.shape
    blocks, size = place.shape[:2]
    peer = size // n_data
    wide = width + offsets.shape[1]
    if size % 16:
        rows = jnp.concatenate([add(mine, other), offsets], axis=1).reshape(blocks, size, wide)
        moved = jnp.einsum("bsr,brw->bsw", place, rows, preferred_element_type=F32).astype(BF)
        return moved.reshape(blocks, n_data, peer, wide).swapaxes(0, 1).reshape(n_data, -1, wide)

    def body(mine_ref, other_ref, place_ref, offsets_ref, result):
        moved, beside = [], []
        for b in range(blocks):
            span = slice(b * size, (b + 1) * size)
            moved.append(dot(place_ref[b], add(mine_ref[span], other_ref[span])))
            beside.append(dot(place_ref[b], offsets_ref[span]))
        for d in range(n_data):
            part = slice(d * peer, (d + 1) * peer)
            result[d, :, :width] = jnp.concatenate([m[part] for m in moved], axis=0).astype(BF)
            result[d, :, width:] = jnp.concatenate([m[part] for m in beside], axis=0).astype(BF)

    return local_kernel(
        body,
        [jax.ShapeDtypeStruct((n_data, blocks * peer, wide), BF)],
        [mine, other, place, offsets],
        (),
        count * size * wide,
    )[0]


def embed_rows(pieces, texts, gain, peer):
    n_data, stack, wide = pieces[0].shape
    count, width = texts[0].shape
    blocks = len(texts)
    total_rows, total = n_data * stack, blocks * count

    def in_order(piece, p):
        order = [p ^ b for b in range(blocks)]
        return piece if p == 0 else jnp.concatenate([piece[o * peer : (o + 1) * peer] for o in order], axis=0)

    def math(parts, text, gain_row):
        rows = parts[0][:, :width]
        for part in parts[1:]:
            rows = rows + part[:, :width]
        line = lax.broadcasted_iota(jnp.int32, (total_rows, 1), 0)
        target = parts[0][:, width : width + 1] + (line // peer % blocks * count).astype(F32)
        spots = lax.broadcasted_iota(jnp.int32, (1, total), 1).astype(F32) == target
        spots = spots.astype(F32)
        turned = (((0,), (0,)), ((), ()))
        placed = lax.dot_general(spots.astype(BF), rows.astype(BF), turned, preferred_element_type=F32)
        named = lax.dot_general(spots, jnp.ones_like(target), turned, preferred_element_type=F32)
        embed = jnp.where(named > 0.5, placed, text.astype(F32))
        meansq = jnp.mean(embed * embed, axis=-1, keepdims=True) + 1e-06
        return embed[:count], (embed * lax.rsqrt(meansq) * gain_row).astype(BF)

    gain = gain.reshape(1, width)
    if stack % 8:
        parts = [
            jnp.concatenate([in_order(piece[d], p) for d in range(n_data)], axis=0).astype(F32)
            for p, piece in enumerate(pieces)
        ]
        return math(parts, jnp.concatenate(texts, axis=0), gain)

    def body(*refs):
        gain_ref, embed_ref, normed_ref = refs[2 * blocks :]
        parts = [
            jnp.concatenate([in_order(ref[d].astype(F32), p) for d in range(n_data)], axis=0)
            for p, ref in enumerate(refs[:blocks])
        ]
        text = jnp.concatenate([ref[...].astype(F32) for ref in refs[blocks : 2 * blocks]], axis=0)
        embed_ref[...], normed_ref[...] = math(parts, text, gain_ref[...])

    return local_kernel(
        body,
        [out(count, width, F32), out(total, width)],
        [*pieces, *texts, gain],
        (),
        total * total_rows * width,
    )


def pick_rows(picks, pieces, starts, sizes):
    count, width = sum(p.shape[0] for p in pieces), pieces[0].shape[1]
    if not fits(pieces) or any(n % 8 for n in (*starts, *sizes)):
        rows = dot(picks, jnp.concatenate(pieces, axis=0)).astype(BF)
        return [rows[at : at + size] for at, size in zip(starts, sizes)]

    def body(*refs):
        n = len(pieces)
        whole = refs[-1]
        put_together(refs[1 : n + 1], whole)
        rows = dot(refs[0][...], whole[...])
        for ref, at, size in zip(refs[n + 1 : -1], starts, sizes):
            ref[...] = rows[at : at + size].astype(BF)

    return local_kernel(
        body,
        [out(size, width) for size in sizes],
        [picks, *pieces],
        [pltpu.VMEM((count, width), BF)],
        picks.shape[0] * count * width,
    )


def combine_rows(total, coef, backs, starts, dtype, cuts):
    count, width = total.shape
    slots = coef.shape[2]
    ends = list(starts[1:]) + [slots]
    if any(n % 16 for n in (slots, *starts)):
        whole = jnp.concatenate(
            [jnp.pad(b, ((0, e - s - b.shape[0]), (0, 0))) for b, s, e in zip(backs, starts, ends)],
            axis=0,
        )
        value = (total + dot(coef[0], whole) + dot(coef[1], whole)).astype(dtype)
        return jnp.split(value, cuts, axis=1)

    def body(*refs):
        total_ref, coef_ref, whole = refs[0], refs[1], refs[-1]
        for ref, at, end in zip(refs[2 : 2 + len(backs)], starts, ends):
            size = ref.shape[0]
            if size != end - at:
                whole[end - 16 : end] = jnp.zeros((16, width), BF)
            whole[at : at + size] = ref[...]
        rows = whole[...]
        value = total_ref[...] + dot(coef_ref[0], rows)
        value = (value + dot(coef_ref[1], rows)).astype(dtype)
        step = width // cuts
        for i, result in enumerate(refs[2 + len(backs) : -1]):
            result[...] = value[:, i * step : (i + 1) * step]

    return local_kernel(
        body,
        [out(count, width // cuts, dtype)] * cuts,
        [total, coef, *backs],
        [pltpu.VMEM((slots, width), BF)],
        2 * count * width * slots,
    )


def one_hot(places, count):
    return places[None, :] == jnp.arange(count, dtype=jnp.int32)[:, None]


def shards(
    text_embed,
    image_feats,
    tile_pos,
    proj_in,
    proj_out,
    norm_gain,
    shared_gate,
    shared_up,
    shared_down,
    expert_gate,
    expert_up,
    expert_down,
    route_ids,
    route_wts,
):
    tok_dev, width = text_embed.shape
    img_dev = image_feats.shape[0]
    n_data = lax.axis_size("dp")
    n_group = lax.axis_size("expert")
    peer = img_dev // n_data
    my_place = lax.axis_index("expert")
    top = route_ids.shape[1]
    group_rows = tok_dev * n_group
    capacity = 3 * group_rows * top // (2 * n_data)
    share = capacity // n_group

    weights_in, weights_out, own_feats = fetch(proj_in, proj_out, image_feats)
    routes = spread(jnp.concatenate([route_ids, route_wts], axis=1))
    spots, feats = spread(tile_pos), spread(image_feats)
    partner = [swap(image_feats, "expert", 1)]
    feats, partner, spots, routes, own_feats = fence(feats, partner, spots, routes, own_feats)
    feats = feats + partner + [swap(p, "expert", 1) for p in feats[1:]]
    keep, give = image_rows([own_feats, *feats[1:]], weights_in, weights_out)

    spots, keep, give = fence(spots, keep, give)
    spots = jnp.stack(spots)
    owner = spots // tok_dev // n_group
    earlier = jnp.arange(img_dev)[None, :] < jnp.arange(img_dev)[:, None]
    rank_img = jnp.sum(((owner[:, :, None] == owner[:, None, :]) & earlier).astype(jnp.int32), axis=2)
    seat = owner * peer + rank_img
    place = (seat[:, None, :] == jnp.arange(img_dev, dtype=jnp.int32)[None, :, None]).astype(BF)
    offsets = jnp.broadcast_to((spots % tok_dev).astype(BF).reshape(-1, 1), (spots.size, 128))
    leaving = place_rows(keep, swap(give, "expert", 1), place, offsets, n_data)
    texts, routes, leaving = fence(text_embed, routes, leaving)
    texts = spread(texts)
    routes = routes + [swap(p, "expert", 1) for p in routes]
    arrived = lax.all_to_all(leaving, "dp", split_axis=0, concat_axis=0, tiled=True)
    texts, routes, arrived = fence(texts, routes, arrived)
    embed_f, normed = embed_rows(spread(arrived), texts, norm_gain, peer)
    normed = [normed, swap(normed, "expert", 1)]

    routes = jnp.concatenate(routes, axis=0)
    ids, weights = routes[:, :top], routes[:, top:].astype(F32)
    weights = weights / jnp.sum(weights, axis=1, keepdims=True)
    rows_at = jnp.arange(group_rows, dtype=jnp.int32)
    token = (my_place ^ reversed_bits(rows_at // tok_dev, n_group)) * tok_dev + rows_at % tok_dev
    named = ids[:, :, None] == jnp.arange(n_data, dtype=jnp.int32)[None, None, :]
    before = token[None, :] < token[:, None]
    counts = dot(before.astype(BF), jnp.any(named, axis=1).astype(BF))
    rank = jnp.sum(jnp.where(named, counts[:, None, :], 0.0), axis=2).astype(jnp.int32)
    distance = ids ^ lax.axis_index("dp")

    half, wide = n_data // 2, capacity // 2
    core, chip, chips = my_place % 2, my_place // 2, n_group // 2
    apart = -(-share // 16) * 16
    mine = rank // wide == core
    block = rank % wide // share
    turned = reversed_bits(block ^ chip, chips) * share + rank % share
    near_slot = distance * wide + jnp.where(distance < 2, rank % wide, turned)
    far_slot = half * wide + (distance - half) * apart + rank % share
    slot = jnp.where(
        distance < half,
        jnp.where(mine, near_slot, -1),
        jnp.where(rank // share == my_place, far_slot, -1),
    )
    sizes = [wide] * half + [share] * (n_data - half)
    starts = [m * wide if m < half else half * wide + (m - half) * apart for m in range(n_data)]
    picks = sum(
        one_hot(slot[:, k], half * wide + (n_data - half) * apart).astype(BF) for k in range(top)
    )

    owned = jnp.where(distance < half, mine & (block == chip), rank // share == my_place)
    back_slot = jnp.where(
        distance < 2,
        jnp.where(mine, distance * wide + rank % wide, -1),
        jnp.where(owned, 2 * wide + (distance - 2) * apart + rank % share, -1),
    )
    back_starts = [m * wide if m < 2 else 2 * wide + (m - 2) * apart for m in range(n_data)]
    hits = [one_hot(back_slot[:, k], 2 * wide + (n_data - 2) * apart) for k in range(top)]
    coef = sum(jnp.where(hit, weights[:, k][None, :], 0.0) for k, hit in enumerate(hits)).T
    coef_hi = coef.astype(BF)
    coef = jnp.stack([coef_hi, (coef - coef_hi.astype(F32)).astype(BF)])

    send = pick_rows(picks, normed, starts, sizes)
    got = [None] * n_data
    got[0] = send[0]
    quarter = n_data // 4
    near, far_one, far_two = range(half), range(half, half + quarter), range(half + quarter, n_data)

    def join(stage):
        return jnp.concatenate([got[m] for m in stage], axis=0)

    def both(pieces):
        return pieces + [swap(p, "expert", 1) for p in pieces]

    for m in (*near[1:], *far_one):
        got[m] = swap(send[m], "dp", m)
    one, send = fence(join(far_one), send)

    for m in far_two:
        got[m] = swap(send[m], "dp", m)
    one, got = fence(spread(one), got)

    experts = (expert_gate[0].T, expert_up[0].T, expert_down[0])
    one_keep, one_give = expert_rows(both(one), *experts)
    two, one_keep, one_give = fence(spread(join(far_two)), one_keep, one_give)
    two_keep, two_give = expert_rows(both(two), *experts)
    mine = join(near)
    mine = [mine, swap(mine, "expert", 1)]
    mine, two_keep = fence(mine, two_keep)
    order = [(0, 2 * wide)]
    order += [(m * wide + p * share, share) for p in range(chips) for m in near[2:]]
    keep, give = expert_rows(mine, *experts, order)
    one = sum_rest(add(one_keep, swap(one_give, "expert", 1)))
    one, keep, give, normed = fence(one, keep, give, normed)
    two = sum_rest(add(two_keep, swap(two_give, "expert", 1)))
    rows = add(keep, swap(give, "expert", 1))
    rest = sum_rest(rows[2 * wide :])

    def send_back(m, rows, at, size):
        part = rows[at : at + size]
        return swap(part, "dp", m) if m else part

    back = [send_back(m, rows, m * wide, wide) for m in near[:2]]
    rest, two = fence(rest, two)
    back += [send_back(m, rest, i * share, share) for i, m in enumerate(near[2:])]
    back += [send_back(m, one, i * share, share) for i, m in enumerate(far_one)]
    back += [send_back(m, two, i * share, share) for i, m in enumerate(far_two)]
    shared = shared_rows(normed, shared_gate.T, shared_up.T, shared_down)

    middle = group_rows // 2
    keep, give = [
        combine_rows(part, coef[:, rows], back, back_starts, BF, 2)
        for part, rows in zip(shared, (slice(0, middle), slice(middle, None)))
    ]
    total = [sum_rest(add(k, swap(g, "expert", 1))) for k, g in zip(keep, give)]
    return (embed_f + jnp.concatenate(total, axis=1).astype(F32)).astype(BF)


def solution(mesh):
    return jax.shard_map(
        shards,
        mesh=mesh,
        in_specs=(
            P(("dp", "expert"), None),
            P(("dp", "expert"), None),
            P(("dp", "expert")),
            P(None, "expert"),
            P("expert", None),
            P(),
            P(None, "expert"),
            P(None, "expert"),
            P("expert", None),
            P("dp", None, "expert"),
            P("dp", None, "expert"),
            P("dp", "expert", None),
            P(("dp", "expert"), None),
            P(("dp", "expert"), None),
        ),
        out_specs=P(("dp", "expert"), None),
        check_vma=False,
    )
```
